32 devices in a mesh: comp: 2 (over x), lat: 4 (over y, core), lon: 4 (over z).
Axes of the slice: x: 2, y: 2, z: 4, core: 2. Of those that a mesh axis runs over, the one named last changes fastest.
Arguments:
- state: bfloat16 [2, 80, 8, 1024], P('comp', None, 'lat', 'lon'), may hold values from -6 to 6
- direction: bfloat16 [2, 80, 8, 1024], P('comp', None, 'lat', 'lon'), may hold values from -6 to 6
- air_first: bfloat16 [9, 512, 80], replicated, may hold values from -0.21875 to 0.21875
- air_bias: float32 [512], replicated, may hold values from -4 to 4
- air_second: bfloat16 [9, 80, 512], replicated, may hold values from -0.09375 to 0.09375
- air_flux: bfloat16 [2, 80], replicated, may hold values from -1.25 to 1.25
- aloft_reaction_to_seawarmth: float32 [80], replicated, may hold values from -4 to 4
- sea_first: bfloat16 [9, 256, 40], replicated, may hold values from -0.3125 to 0.3125
- sea_bias: float32 [256], replicated, may hold values from -4 to 4
- sea_second: bfloat16 [9, 40, 256], replicated, may hold values from -0.125 to 0.125
- sea_forcing: bfloat16 [40, 2], replicated, may hold values from -4 to 4
- regrid_index: int32 [2, 8, 8, 1024], P('comp', None, 'lat', 'lon'), may hold values from 0 to 2047, as said below
- regrid_weight: int32 [2, 8, 8, 1024], P('comp', None, 'lat', 'lon'), may hold values from 1 to 255
- land_mask: int32 [2, 8, 1024], P(None, 'lat', 'lon'), may hold values 0 or 1
Outputs:
- image: bfloat16 [2, 80, 8, 1024], P('comp', None, 'lat', 'lon')
- product: bfloat16 [2, 80, 8, 1024], P('comp', None, 'lat', 'lon')
The draws below stay inside these ranges and needn't reach their ends.
Inputs may be any that keep to these rules, and one draw needn't show every extreme that they name: `regrid_index`: in block 0, entries number cells of the fine window of the tile that holds the cell (below 2048); in block 1 they number cells of its coarse window (below 1024); the sources of a cell lie near it.
All inputs are finite; a program needn't handle non-finite values. No bound on the sum of `land_mask` on one device may be relied on, other than what follows from the above.
Results may differ from the reference program's by a relative error of at most 0.0064.
Values may be sent and summed in bfloat16 or wider, within the bound.
A program may use at most 64 MiB of HBM per device.

```python
import jax
import jax.numpy as jnp
from jax import lax

CH_ATM = 80
HID_ATM = 512
CH_OCN = 40
HID_OCN = 256
FLUX = 2
SLOTS = 8
ROWS_DEV = 2
COLS_DEV = 256
NLAT = 8
NLON = 1024
N_LAT = 4
N_LON = 4


def draw_regrid_index(key, part):
    rows = ROWS_DEV
    columns = COLS_DEV
    first_key, second_key = jax.random.split(jax.random.fold_in(key, 17))
    local_row = (lax.iota(jnp.int32, NLAT) % rows)[:, None]
    local_col = (lax.iota(jnp.int32, NLON) % columns)[None, :]
    air_offset = jax.random.randint(first_key, (NLAT, NLON), 1, columns - 1)
    air_offset = jnp.where(local_col == 0, 1, jnp.where(local_col == columns - 1, columns - 2, air_offset))
    sea_offset = jax.random.randint(second_key, (NLAT, NLON), 1, columns + 1)
    sea_offset = jnp.where(local_col == 0, 1, jnp.where(local_col == columns - 1, columns, sea_offset))
    slot = lax.iota(jnp.int32, 8)[:, None, None]
    air_row = 2 * local_row + slot // 4
    air_col = local_col + air_offset - 1 + slot % 4
    aloft_lookup_position = air_row * 2 * columns + air_col
    fine_row = slot // 4 * rows + local_row
    sea_row = jnp.minimum(fine_row // 2 + slot % 4 // 2, rows - 1)
    sea_col = local_col + sea_offset - 1 + slot % 2
    sea_index = sea_row * 2 * columns + sea_col
    return jnp.stack([aloft_lookup_position, sea_index]).astype(jnp.int32)


def plant(entries, stream_key, low, high):
    longest = entries.shape.index(max(entries.shape))
    spots = []
    for shift in (0, 1):
        where = [jax.random.randint(jax.random.fold_in(stream_key, axis), (), 0, length) for axis, length in enumerate(entries.shape)]
        where[longest] = (where[longest] + shift) % entries.shape[longest]
        spots.append(tuple(where))
    return entries.at[spots[0]].set(low).at[spots[1]].set(high)


def block_levels(rng, dims, cuts, low, top_value):
    gain, own = 1.0, jax.random.fold_in(rng, 6)
    for axis_at, blocks in cuts:
        draws = jnp.exp(jax.random.uniform(jax.random.fold_in(own, axis_at), (blocks,), jnp.float32, low / len(cuts), top_value / len(cuts)))
        gain = gain * jnp.repeat(draws, dims[axis_at] // blocks).reshape([-1 if axis == axis_at else 1 for axis in range(len(dims))])
    return gain


def bell_draw(stream_key, dims, scale, reach, cuts=(), kind=jnp.bfloat16):
    array = scale * jax.random.normal(stream_key, dims, jnp.float32)
    if cuts:
        array = array * block_levels(stream_key, dims, cuts, -0.22, 0.18)
    return jnp.clip(array, -reach, reach).astype(kind)


def setup_inputs(seed: int = 0) -> dict:
    splits = jax.random.split(jax.random.key(seed), 15)
    return {
        "state": bell_draw(splits[0], (2, CH_ATM, NLAT, NLON), 1.0, 6.0, ((0, 2), (2, 4), (3, 4))),
        "direction": bell_draw(splits[1], (2, CH_ATM, NLAT, NLON), 1.0, 6.0, ((0, 2), (2, 4), (3, 4))),
        "air_first": bell_draw(splits[2], (9, HID_ATM, CH_ATM), (9 * CH_ATM) ** -0.5, 0.21875),
        "air_bias": bell_draw(splits[3], (HID_ATM,), 1.0, 4.0, (), jnp.float32),
        "air_second": bell_draw(splits[4], (9, CH_ATM, HID_ATM), (9 * HID_ATM) ** -0.5, 0.09375),
        "air_flux": bell_draw(splits[5], (FLUX, CH_ATM), (CH_ATM // 4) ** -0.5, 1.25),
        "aloft_reaction_to_seawarmth": bell_draw(splits[6], (CH_ATM,), 1.0, 4.0, (), jnp.float32),
        "sea_first": bell_draw(splits[7], (9, HID_OCN, CH_OCN), (9 * CH_OCN) ** -0.5, 0.3125),
        "sea_bias": bell_draw(splits[8], (HID_OCN,), 1.0, 4.0, (), jnp.float32),
        "sea_second": bell_draw(splits[9], (9, CH_OCN, HID_OCN), (9 * HID_OCN) ** -0.5, 0.125),
        "sea_forcing": bell_draw(splits[10], (CH_OCN, FLUX), FLUX ** -0.5, 4.0),
        "regrid_index": draw_regrid_index(jax.random.fold_in(splits[14], 71), 0),
        "regrid_weight": plant(jax.random.randint(splits[12], (2, SLOTS, NLAT, NLON), 1, 256), jax.random.fold_in(splits[12], 1), 1, 255).astype(jnp.int32),
        "land_mask": plant((jax.random.randint(splits[13], (2, NLAT, NLON), 0, 4) < 3).astype(jnp.int32), jax.random.fold_in(splits[13], 1), 0, 1),
    }


HIGH = lax.Precision.HIGHEST


def pad_grid(field):
    field = jnp.pad(field, ((0, 0), (1, 1), (0, 0)))
    return jnp.concatenate([field[:, :, -1:], field, field[:, :, :1]], axis=2)


def conv_taps(weight, field):
    padded = pad_grid(field.astype(jnp.float32))
    height = field.shape[1]
    length = field.shape[2]
    summed = jnp.zeros((weight.shape[1], height, length), jnp.float32)
    for tap in range(9):
        down_off, across_off = divmod(tap, 3)
        part = padded[:, down_off:down_off + height, across_off:across_off + length]
        summed = summed + jnp.einsum("oc,chw->ohw", weight[tap].astype(jnp.float32), part)
    return summed


def conv_back(weight, field):
    padded = pad_grid(field.astype(jnp.float32))
    height = field.shape[1]
    length = field.shape[2]
    summed = jnp.zeros((weight.shape[2], height, length), jnp.float32)
    for tap in range(9):
        down_off, across_off = divmod(tap, 3)
        part = padded[:, 2 - down_off:2 - down_off + height, 2 - across_off:2 - across_off + length]
        summed = summed + jnp.einsum("oc,ohw->chw", weight[tap].astype(jnp.float32), part)
    return summed


def fine_from_packed(packed):
    half = packed.shape[0] // 2
    split = packed.reshape(2, half, N_LAT, ROWS_DEV, NLON).transpose(1, 2, 0, 3, 4)
    return split.reshape(half, 2 * NLAT, NLON)


def packed_from_fine(fine):
    half = fine.shape[0]
    split = fine.reshape(half, N_LAT, 2, ROWS_DEV, NLON).transpose(2, 0, 1, 3, 4)
    return split.reshape(2 * half, NLAT, NLON)


def tiles(field):
    depth = field.shape[1] // N_LAT
    return field.reshape(field.shape[0], N_LAT, depth, N_LON, COLS_DEV).transpose(0, 1, 3, 2, 4)


def untiles(blocks):
    return blocks.transpose(0, 1, 3, 2, 4).reshape(blocks.shape[0], N_LAT * blocks.shape[3], NLON)


def windows(field):
    blocks = tiles(field)
    joined = jnp.concatenate([blocks, jnp.roll(blocks, -1, axis=2)], axis=4)
    return joined.reshape(field.shape[0], N_LAT, N_LON, -1)


def table_view(table):
    return tiles(table).transpose(1, 2, 0, 3, 4)


def outgoing_marine_flux(fine, index, weight):
    window = windows(fine[None])[0]
    taken = jnp.take_along_axis(window, index.reshape(N_LAT, N_LON, -1), axis=2).reshape(index.shape)
    result = jnp.sum(weight * taken, axis=2) / jnp.sum(weight, axis=2)
    return untiles(result[None])[0]


def to_sea(coarse, index, weight):
    count = coarse.shape[0]
    window = windows(coarse)
    flat_index = jnp.broadcast_to(index.reshape(N_LAT, N_LON, -1)[None], (count, N_LAT, N_LON, index[0, 0].size))
    taken = jnp.take_along_axis(window, flat_index, axis=3)
    taken = taken.reshape(count, N_LAT, N_LON, 2, 4, ROWS_DEV, COLS_DEV)
    grouped = weight.reshape(N_LAT, N_LON, 2, 4, ROWS_DEV, COLS_DEV)
    result = jnp.sum(grouped * taken, axis=4) / jnp.sum(grouped, axis=3)
    result = result.transpose(0, 1, 3, 4, 2, 5)
    return result.reshape(count, 2 * NLAT, NLON)


def arriving_aloft_flux(topmost_marine_level, index, weight):
    values = tiles(topmost_marine_level[None])[0]
    share = weight / jnp.sum(weight, axis=2, keepdims=True) * values[:, :, None]
    size = 4 * ROWS_DEV * COLS_DEV
    offsets = (jnp.arange(N_LAT * N_LON, dtype=jnp.int32) * size).reshape(N_LAT, N_LON, 1, 1, 1)
    flat_index = (index + offsets).reshape(-1).astype(jnp.int32)
    summed = jnp.zeros((N_LAT * N_LON * size,), jnp.float32).at[flat_index].add(share.reshape(-1))
    summed = summed.reshape(N_LAT, N_LON, 2 * ROWS_DEV, 2 * COLS_DEV)
    joined = summed[..., :COLS_DEV] + jnp.roll(summed[..., COLS_DEV:], 1, axis=1)
    return untiles(joined[None])[0]


def from_sea(pulled, index, weight):
    count = pulled.shape[0]
    values = pulled.reshape(count, N_LAT, 2, ROWS_DEV, N_LON, COLS_DEV).transpose(0, 1, 4, 2, 3, 5)
    grouped = weight.reshape(N_LAT, N_LON, 2, 4, ROWS_DEV, COLS_DEV)
    share = (grouped / jnp.sum(grouped, axis=3, keepdims=True))[None] * values[:, :, :, :, None]
    size = 2 * ROWS_DEV * COLS_DEV
    offsets = (jnp.arange(N_LAT * N_LON, dtype=jnp.int32) * size).reshape(N_LAT, N_LON, 1, 1, 1)
    flat_index = (index + offsets).reshape(-1).astype(jnp.int32)
    summed = jnp.zeros((count, N_LAT * N_LON * size), jnp.float32).at[:, flat_index].add(share.reshape(count, -1))
    summed = summed.reshape(count, N_LAT, N_LON, ROWS_DEV, 2 * COLS_DEV)
    joined = summed[..., :COLS_DEV] + jnp.roll(summed[..., COLS_DEV:], 1, axis=2)
    return untiles(joined)


def reference(state, direction, air_first, air_bias, air_second, air_flux, aloft_reaction_to_seawarmth, sea_first, sea_bias, sea_second, sea_forcing, regrid_index, regrid_weight, land_mask):
    aloft_lookup_position = table_view(regrid_index[0])
    aloft_regrid_coefficient = table_view(regrid_weight[0]).astype(jnp.float32)
    sea_index = table_view(regrid_index[1])
    sea_weight = table_view(regrid_weight[1]).astype(jnp.float32)
    sea_state = fine_from_packed(state[1])
    marine_probe_vector = fine_from_packed(direction[1])
    mask = land_mask.reshape(2, N_LAT, ROWS_DEV, NLON).transpose(1, 0, 2, 3).reshape(2 * NLAT, NLON).astype(jnp.float32)

    air_slope = 1.0 - jnp.tanh(conv_taps(air_first, state[0]) + air_bias[:, None, None]) ** 2
    air_hidden = (air_slope * conv_taps(air_first, direction[0])).astype(jnp.bfloat16)
    aloft_perturbation = conv_taps(air_second, air_hidden)
    flux = jnp.einsum("fc,chw->fhw", air_flux.astype(jnp.float32), aloft_perturbation, precision=HIGH)

    sea_slope = 1.0 - jnp.tanh(conv_taps(sea_first, sea_state) + sea_bias[:, None, None]) ** 2
    sea_hidden = (sea_slope * conv_taps(sea_first, marine_probe_vector)).astype(jnp.bfloat16)
    sea_increment = conv_taps(sea_second, sea_hidden)

    seawarmth_lifted = outgoing_marine_flux(marine_probe_vector[0].astype(jnp.float32), aloft_lookup_position, aloft_regrid_coefficient)
    aloft_picture_values = (aloft_perturbation + aloft_reaction_to_seawarmth[:, None, None] * seawarmth_lifted).astype(jnp.bfloat16)
    forcing = to_sea(flux, sea_index, sea_weight)
    added = jnp.einsum("cf,fhw->chw", sea_forcing.astype(jnp.float32), forcing, precision=HIGH)
    sea_image = (mask * (sea_increment + added)).astype(jnp.bfloat16)
    image = jnp.stack([aloft_picture_values, packed_from_fine(sea_image)])

    topmost_marine_level = jnp.einsum("c,chw->hw", aloft_reaction_to_seawarmth, aloft_picture_values.astype(jnp.float32), precision=HIGH)
    pulled = jnp.einsum("cf,chw->fhw", sea_forcing.astype(jnp.float32), sea_image.astype(jnp.float32), precision=HIGH)
    flux_back = from_sea(pulled, sea_index, sea_weight)
    seawarmth_adjoint = arriving_aloft_flux(topmost_marine_level, aloft_lookup_position, aloft_regrid_coefficient)

    pushed = jnp.einsum("fc,fhw->chw", air_flux.astype(jnp.float32), flux_back, precision=HIGH)
    air_cot = (aloft_picture_values.astype(jnp.float32) + pushed).astype(jnp.bfloat16)
    air_back = (air_slope * conv_back(air_second, air_cot)).astype(jnp.bfloat16)
    air_product = conv_back(air_first, air_back).astype(jnp.bfloat16)
    sea_back = (sea_slope * conv_back(sea_second, sea_image)).astype(jnp.bfloat16)
    marine_sensitivity = conv_back(sea_first, sea_back)
    marine_sensitivity = marine_sensitivity.at[0].add(seawarmth_adjoint)
    product = jnp.stack([air_product, packed_from_fine(marine_sensitivity.astype(jnp.bfloat16))])
    return image, product
```

```python
import functools

import jax
import jax.numpy as jnp
from jax import lax
from jax.experimental import pallas as pl
from jax.experimental.pallas import tpu as pltpu
from jax.sharding import PartitionSpec as P

MESH = pl.DeviceIdType.MESH
F32 = jnp.float32
BF16 = jnp.bfloat16
LANES = 128
TILE_WAYS = ((-1, 0), (1, 0))
EDGE_WAYS = ((0, -1), (0, 1), (-1, -1), (-1, 1), (1, -1), (1, 1))
WAYS = TILE_WAYS + EDGE_WAYS


def dot(a, b):
    return jnp.dot(a, b, preferred_element_type=F32)


def split_dot(a, b, dims):
    high = a.astype(BF16)
    low = (a - high.astype(F32)).astype(BF16)
    both = lax.dot_general(
        jnp.concatenate([high, low], axis=0), b, (dims, ((), ())), preferred_element_type=F32
    )
    return both[: a.shape[0]] + both[a.shape[0] :]


def pack_edges(tile, rows, columns):
    lane = lax.broadcasted_iota(jnp.int32, (tile.shape[0], LANES), 1)
    packed = None
    for r in range(rows):
        first = tile[:, r * columns : r * columns + LANES]
        last = tile[:, (r + 1) * columns - LANES : (r + 1) * columns]
        part = jnp.where(lane < 2, first, jnp.where(lane >= LANES - 2, last, 0.0))
        if r:
            part = pltpu.roll(part, LANES // rows * r, 1)
        packed = part if packed is None else packed + part
    return packed


def wide_row(main, left, right, r, rows):
    lane = lax.broadcasted_iota(jnp.int32, left.shape, 1)
    if r:
        back = LANES - LANES // rows * r
        left, right = pltpu.roll(left, back, 1), pltpu.roll(right, back, 1)
    side = jnp.where(lane < 2, right, jnp.where(lane >= LANES - 2, left, 0.0))
    return jnp.concatenate([main, side], axis=1)


def three(row, forward):
    width = row.shape[1]
    before, after = pltpu.roll(row, 1, 1), pltpu.roll(row, width - 1, 1)
    parts = [before, row, after] if forward else [after, row, before]
    return jnp.concatenate(parts, axis=0)


def fold_three(stack, forward, columns):
    k = stack.shape[0] // 3
    width = stack.shape[1]
    first, mid, last = stack[:k], stack[k : 2 * k], stack[2 * k :]
    one, other = (1, width - 1) if forward else (width - 1, 1)
    return (pltpu.roll(first, one, 1) + mid + pltpu.roll(last, other, 1))[:, :columns]


def kernel(
    cfg,
    inp,
    tab,
    par,
    aw1, aw1t, aw2, aw2t,
    sw1, sw1t, sw2, sw2t,
    image_ref,
    product_ref,
    edge_a, tiles_a, edges_a,
    cot, edge_b, tiles_b, edges_b,
    pay, paid, out_win, in_win,
    onehot, share_hi, values,
    ax, av, aslope, az,
    sx, sv, sslope, sz,
    send_a, recv_a, send_b, recv_b, send_c, recv_c, send_d, recv_d,
):
    rows, columns, lat_n, lon_n, air_k, air_h, sea_k, sea_h = cfg
    cells = rows * columns
    comp, lat, lon = (lax.axis_index(a) for a in ("comp", "lat", "lon"))
    is_air = comp == 0
    is_sea = comp == 1
    mine = {"comp": comp, "lat": lat, "lon": lon}
    del mine

    def exists(dl):
        return lat + dl >= 0 if dl < 0 else lat + dl < lat_n

    def there(dl, dn):
        return (comp, (lat + dl + lat_n) % lat_n, (lon + dn + lon_n) % lon_n)

    def across(dn):
        return (1 - comp, lat, (lon + dn + lon_n) % lon_n)

    def when(dl, act):
        if dl == 0:
            act()
        else:
            pl.when(exists(dl))(act)

    barrier = pltpu.get_barrier_semaphore()
    for dl, dn in WAYS:
        when(dl, lambda dl=dl, dn=dn: pl.semaphore_signal(
            barrier, inc=1, device_id=there(dl, dn), device_id_type=MESH))
    for dn in (-1, 0, 1):
        pl.semaphore_signal(barrier, inc=1, device_id=across(dn), device_id_type=MESH)

    def halo(tile, edge, tiles, edges, send, recv):
        copies = []
        for i, (dl, dn) in enumerate(WAYS):
            n = i - len(TILE_WAYS)
            copies.append(pltpu.make_async_remote_copy(
                src_ref=tile if n < 0 else edge,
                dst_ref=tiles.at[i] if n < 0 else edges.at[n],
                send_sem=send.at[i], recv_sem=recv.at[i],
                device_id=there(dl, dn), device_id_type=MESH))
        return copies

    def clear(tiles, edges):
        for i, (dl, dn) in enumerate(WAYS):
            n = i - len(TILE_WAYS)

            def act(i=i, n=n):
                if n < 0:
                    tiles[i] = jnp.zeros(tiles.shape[1:], BF16)
                else:
                    edges[n] = jnp.zeros(edges.shape[1:], BF16)

            if dl:
                pl.when(jnp.logical_not(exists(-dl)))(act)

    def start(copies):
        for (dl, dn), c in zip(WAYS, copies):
            when(dl, c.start)

    def wait_recv(copies):
        for (dl, dn), c in zip(WAYS, copies):
            when(-dl, c.wait_recv)

    def wait_send(copies):
        for (dl, dn), c in zip(WAYS, copies):
            when(dl, c.wait_send)

    halo_a = halo(inp, edge_a, tiles_a, edges_a, send_a, recv_a)
    halo_b = halo(cot, edge_b, tiles_b, edges_b, send_b, recv_b)
    pays = [pltpu.make_async_remote_copy(
        src_ref=pay, dst_ref=paid.at[i], send_sem=send_c.at[i], recv_sem=recv_c.at[i],
        device_id=across(dn), device_id_type=MESH) for i, dn in enumerate((0, -1))]
    wins = [pltpu.make_async_remote_copy(
        src_ref=out_win, dst_ref=in_win.at[i], send_sem=send_d.at[i], recv_sem=recv_d.at[i],
        device_id=across(dn), device_id_type=MESH) for i, dn in enumerate((0, 1))]

    edge_a[...] = pack_edges(inp[...].astype(F32), rows, columns).astype(BF16)
    pay[...] = jnp.zeros(pay.shape, F32)

    @pl.when(is_sea)
    def _():
        base = 2 * sea_k
        centre = inp[base : 2 * base, :].astype(F32)
        pay[0:1, :] = centre[0:1]
        pay[1:2, :] = centre[sea_k : sea_k + 1]

    up = jnp.where(exists(-1), 3, 0)
    down = jnp.where(exists(1), 3, 0)
    pl.semaphore_wait(barrier, 5 + up + down)
    start(halo_a)

    @pl.when(is_sea)
    def _():
        for c in pays:
            c.start()

    clear(tiles_a, edges_a)
    clear(tiles_b, edges_b)

    code = tab[0:8, :]
    index = code // 256
    weight = (code % 256).astype(F32)
    near = jnp.sum(weight[0:4], axis=0, keepdims=True)
    far = jnp.sum(weight[4:8], axis=0, keepdims=True)
    slot8 = lax.broadcasted_iota(jnp.int32, weight.shape, 0)
    total = jnp.where(is_air, near + far, jnp.where(slot8 < 4, near, far))
    share = weight / total
    high = index // LANES
    low = index % LANES
    place = lax.broadcasted_iota(jnp.int32, (LANES, cells), 0)
    wrows = values.shape[0]
    row16 = lax.broadcasted_iota(jnp.int32, (wrows, cells), 0)
    row16 = jnp.where(is_air, row16, row16 % (wrows // 2))
    for s in range(8):
        onehot[:, s * cells : (s + 1) * cells] = jnp.where(
            place == low[s : s + 1], 1.0, 0.0).astype(BF16)
        share_hi[:, s * cells : (s + 1) * cells] = jnp.where(
            row16 == high[s : s + 1], share[s : s + 1], 0.0)

    per = columns // LANES

    def gather():
        for f in range(2):
            for r in range(rows):
                for nxt in range(2):
                    for h in range(per):
                        at = ((f * rows + r) * 2 + nxt) * per + h
                        lane0 = r * columns + h * LANES
                        values[at : at + 1, :] = paid[nxt, f : f + 1, lane0 : lane0 + LANES]
        got = split_dot(values[...], onehot[...], ((1,), (0,))) * share_hi[...]
        parts = [got[:, s * cells : (s + 1) * cells] for s in range(8)]
        return sum(parts[1:4], parts[0]), sum(parts[5:8], parts[4])

    def scatter(first, second):
        spread = jnp.concatenate([first] * 4 + [second] * 4, axis=1) * share_hi[...]
        out_win[...] = split_dot(spread, onehot[...], ((1,), (1,)))

    def arrived():
        fields = []
        for f in range(2):
            pieces = []
            for r in range(rows):
                for h in range(per):
                    own = ((f * rows + r) * 2) * per + h
                    pieces.append(in_win[0, own : own + 1, :] + in_win[1, own + per : own + per + 1, :])
            fields.append(jnp.concatenate(pieces, axis=1))
        return fields

    def place_of(q, split):
        height = rows * split
        where = -1 if q < 0 else (1 if q >= height else 0)
        q = q - where * height
        return where, q // rows, q % rows

    def stacks(tile, tiles, edges, base, k, split, forward, dst):
        lo, hi = base, base + k * split
        own = tile[lo:hi, :].astype(F32)
        above, below = tiles[1, lo:hi, :].astype(F32), tiles[0, lo:hi, :].astype(F32)
        edge = [edges[n, lo:hi, :].astype(F32) for n in range(6)]
        lefts = {0: edge[1], -1: edge[5], 1: edge[3]}
        rights = {0: edge[0], -1: edge[4], 1: edge[2]}
        mains = {0: own, -1: above, 1: below}
        for p in range(rows * split + 4):
            where, s, r = place_of(p - 2, split)
            ch = slice(s * k, (s + 1) * k)
            row = wide_row(mains[where][ch, r * columns : (r + 1) * columns],
                           lefts[where][ch], rights[where][ch], r, rows)
            dst[p] = three(row, forward).astype(BF16)

    def keep(p, height):
        gone = ((p == 0) & (lat == 0)) | ((p == height + 1) & (lat == lat_n - 1))
        return jnp.where(gone, 0.0, 1.0)

    def first_conv(w1, bias, x, v, slope, z, height):
        def body(p, carry):
            pre = dot(w1[0], x[p]) + dot(w1[1], x[p + 1]) + dot(w1[2], x[p + 2]) + bias
            t = jnp.tanh(pre)
            s = 1.0 - t * t
            slope[p] = s
            lin = dot(w1[0], v[p]) + dot(w1[1], v[p + 1]) + dot(w1[2], v[p + 2])
            z[p] = (s * keep(p, height) * lin).astype(BF16)
            return carry
        lax.fori_loop(0, height + 2, body, 0)

    def second_conv(w2, z, height):
        return [fold_three(dot(w2[0], z[i]) + dot(w2[1], z[i + 1]) + dot(w2[2], z[i + 2]),
                           True, columns) for i in range(height)]

    def second_back(w2t, c, slope, z, height):
        def body(p, carry):
            lin = dot(w2t[0], c[p + 2]) + dot(w2t[1], c[p + 1]) + dot(w2t[2], c[p])
            z[p] = (slope[p] * keep(p, height) * lin).astype(BF16)
            return carry
        lax.fori_loop(0, height + 2, body, 0)

    def first_back(w1t, z, height):
        return [fold_three(dot(w1t[0], z[i + 2]) + dot(w1t[1], z[i + 1]) + dot(w1t[2], z[i]),
                           False, columns) for i in range(height)]

    def packed(fine, split):
        parts = [jnp.concatenate(fine[s * rows : (s + 1) * rows], axis=1) for s in range(split)]
        return parts

    flux0, flux1 = par[0:air_k, 2:3], par[0:air_k, 3:4]
    react = par[0:air_k, 4:5]
    force0, force1 = par[0:sea_k, 5:6], par[0:sea_k, 6:7]
    half_rows = wrows // 2
    wait_recv(halo_a)

    @pl.when(is_air)
    def _():
        stacks(inp, tiles_a, edges_a, 0, air_k, 1, True, ax)
        stacks(inp, tiles_a, edges_a, air_k, air_k, 1, True, av)
        first_conv(aw1, par[0:air_h, 0:1], ax, av, aslope, az, rows)
        y = packed(second_conv(aw2, az, rows), 1)[0]
        pay[0:1, :] = jnp.sum(flux0 * y, axis=0, keepdims=True)
        pay[1:2, :] = jnp.sum(flux1 * y, axis=0, keepdims=True)
        for c in pays:
            c.start()
        for c in pays:
            c.wait_recv()
        near, far = gather()
        lifted = jnp.sum(near + far, axis=0, keepdims=True)
        image = (y + react * lifted).astype(BF16)
        image_ref[...] = image
        wide = image.astype(F32)
        surface = jnp.sum(react * wide, axis=0, keepdims=True)
        source = jnp.broadcast_to(surface, (wrows, cells))
        scatter(source, source)
        for c in wins:
            c.start()
        for c in wins:
            c.wait_recv()
        back0, back1 = arrived()
        total = wide + (flux0 * back0 + flux1 * back1)
        cot[...] = total.astype(BF16)
        edge_b[...] = pack_edges(cot[...].astype(F32), rows, columns).astype(BF16)

    @pl.when(is_sea)
    def _():
        stacks(inp, tiles_a, edges_a, 0, sea_k, 2, True, sx)
        stacks(inp, tiles_a, edges_a, 2 * sea_k, sea_k, 2, True, sv)
        first_conv(sw1, par[0:sea_h, 1:2], sx, sv, sslope, sz, 2 * rows)
        ys = packed(second_conv(sw2, sz, 2 * rows), 2)
        for c in pays:
            c.wait_recv()
        images, sources = [], []
        row_at = lax.broadcasted_iota(jnp.int32, (wrows, cells), 0)
        for t, got in enumerate(gather()):
            f0 = jnp.sum(got[:half_rows], axis=0, keepdims=True)
            f1 = jnp.sum(got[half_rows:], axis=0, keepdims=True)
            mask = tab[8 + t : 9 + t, :].astype(F32)
            one = (mask * (ys[t] + (force0 * f0 + force1 * f1))).astype(BF16).astype(F32)
            images.append(one)
            pulled0 = jnp.sum(force0 * one, axis=0, keepdims=True)
            pulled1 = jnp.sum(force1 * one, axis=0, keepdims=True)
            sources.append(jnp.where(row_at < half_rows, pulled0, pulled1))
        scatter(*sources)
        for c in wins:
            c.start()
        image = jnp.concatenate(images, axis=0).astype(BF16)
        image_ref[...] = image
        cot[...] = image
        edge_b[...] = pack_edges(image.astype(F32), rows, columns).astype(BF16)

    start(halo_b)
    wait_recv(halo_b)

    @pl.when(is_air)
    def _():
        stacks(cot, tiles_b, edges_b, 0, air_k, 1, False, ax)
        second_back(aw2t, ax, aslope, az, rows)
        product_ref[...] = packed(first_back(aw1t, az, rows), 1)[0].astype(BF16)

    @pl.when(is_sea)
    def _():
        stacks(cot, tiles_b, edges_b, 0, sea_k, 2, False, sx)
        second_back(sw2t, sx, sslope, sz, 2 * rows)
        fine = packed(first_back(sw1t, sz, 2 * rows), 2)
        for c in wins:
            c.wait_recv()
        top = lax.broadcasted_iota(jnp.int32, (sea_k, cells), 0) == 0
        fine = [f + jnp.where(top, b, 0.0) for f, b in zip(fine, arrived())]
        product_ref[...] = jnp.concatenate(fine, axis=0).astype(BF16)

    for c in pays + wins:
        c.wait_send()
    wait_send(halo_a)
    wait_send(halo_b)


def by_row(w):
    taps, o, c = w.shape
    return w.reshape(3, 3, o, c).transpose(0, 2, 1, 3).reshape(3, o, 3 * c)


def shards(
    lat_n, lon_n, state, direction, air_first, air_bias, air_second, air_flux, reaction,
    sea_first, sea_bias, sea_second, sea_forcing, regrid_index, regrid_weight, land_mask,
):
    channels, rows, columns = state.shape[1:]
    cells = rows * columns
    air_h, air_k = air_first.shape[1:]
    sea_h, sea_k = sea_first.shape[1:]
    inp = jnp.concatenate([state[0], direction[0]], axis=0).reshape(2 * channels, cells)
    code = regrid_index[0] * 256 + regrid_weight[0]
    tab = jnp.concatenate([code, land_mask], axis=0).reshape(-1, cells)
    tab = jnp.pad(tab, ((0, -tab.shape[0] % 8), (0, 0)))
    tall = max(air_h, sea_h)

    def column(a):
        return jnp.pad(a.astype(F32), ((0, tall - a.shape[0]), (0, 0)))

    par = jnp.concatenate([
        column(air_bias[:, None]), column(sea_bias[:, None]), column(air_flux.T),
        column(reaction[:, None]), column(sea_forcing), jnp.zeros((tall, 1), F32)], axis=1)
    stacked = lambda w: w.reshape(3, 3 * w.shape[1], w.shape[2])
    flip = lambda w: w.transpose(0, 2, 1)
    weights = []
    for first, second in ((air_first, air_second), (sea_first, sea_second)):
        weights += [by_row(first), stacked(flip(first)), stacked(second), by_row(flip(second))]
    wide = columns + LANES
    wrows = 2 * rows * 2 * columns // LANES
    dma = pltpu.SemaphoreType.DMA
    vmem = pltpu.VMEM
    image, product = pl.pallas_call(
        functools.partial(kernel, (rows, columns, lat_n, lon_n, air_k, air_h, sea_k, sea_h)),
        out_shape=[jax.ShapeDtypeStruct((channels, cells), BF16)] * 2,
        in_specs=[pl.BlockSpec(memory_space=pltpu.VMEM)] * (3 + len(weights)),
        out_specs=[pl.BlockSpec(memory_space=pltpu.VMEM)] * 2,
        scratch_shapes=[
            vmem((2 * channels, LANES), BF16),
            vmem((2, 2 * channels, cells), BF16),
            vmem((6, 2 * channels, LANES), BF16),
            vmem((channels, cells), BF16),
            vmem((channels, LANES), BF16),
            vmem((2, channels, cells), BF16),
            vmem((6, channels, LANES), BF16),
            vmem((8, cells), F32),
            vmem((2, 8, cells), F32),
            vmem((wrows, LANES), F32),
            vmem((2, wrows, LANES), F32),
            vmem((LANES, 8 * cells), BF16),
            vmem((wrows, 8 * cells), F32),
            vmem((wrows, LANES), F32),
            vmem((rows + 4, 3 * air_k, wide), BF16),
            vmem((rows + 4, 3 * air_k, wide), BF16),
            vmem((rows + 2, air_h, wide), F32),
            vmem((rows + 2, air_h, wide), BF16),
            vmem((2 * rows + 4, 3 * sea_k, wide), BF16),
            vmem((2 * rows + 4, 3 * sea_k, wide), BF16),
            vmem((2 * rows + 2, sea_h, wide), F32),
            vmem((2 * rows + 2, sea_h, wide), BF16),
            dma((8,)), dma((8,)), dma((8,)), dma((8,)), dma((2,)), dma((2,)), dma((2,)), dma((2,)),
        ],
        compiler_params=pltpu.CompilerParams(
            collective_id=0, has_side_effects=True, vmem_limit_bytes=48 * 1024 * 1024),
        name="coupled",
    )(inp, tab, par, *weights)
    shape = (1, channels, rows, columns)
    return image.reshape(shape), product.reshape(shape)


def solution(mesh):
    field = P("comp", None, "lat", "lon")
    return jax.shard_map(
        functools.partial(shards, mesh.shape["lat"], mesh.shape["lon"]),
        mesh=mesh,
        in_specs=(field, field) + (P(),) * 9 + (field, field, P(None, "lat", "lon")),
        out_specs=(field, field),
        check_vma=False,
    )
```

```python
import functools

import jax
import jax.numpy as jnp
from jax import lax
from jax.experimental import pallas as pl
from jax.experimental.pallas import tpu as pltpu
from jax.sharding import PartitionSpec as P

MESH = pl.DeviceIdType.MESH
F32 = jnp.float32
BF16 = jnp.bfloat16
LANES = 128
TILE_WAYS = ((-1, 0), (1, 0))
EDGE_WAYS = ((0, -1), (0, 1), (-1, -1), (-1, 1), (1, -1), (1, 1))
WAYS = TILE_WAYS + EDGE_WAYS


def dot(a, b):
    return jnp.dot(a, b, preferred_element_type=F32)


def split_dot(a, b, dims):
    high = a.astype(BF16)
    low = (a - high.astype(F32)).astype(BF16)
    both = lax.dot_general(
        jnp.concatenate([high, low], axis=0), b, (dims, ((), ())), preferred_element_type=F32
    )
    return both[: a.shape[0]] + both[a.shape[0] :]


def pack_edges(tile, rows, columns):
    lane = lax.broadcasted_iota(jnp.int32, (tile.shape[0], LANES), 1)
    packed = None
    for r in range(rows):
        first = tile[:, r * columns : r * columns + LANES]
        last = tile[:, (r + 1) * columns - LANES : (r + 1) * columns]
        part = jnp.where(lane < 2, first, jnp.where(lane >= LANES - 2, last, 0.0))
        if r:
            part = pltpu.roll(part, LANES // rows * r, 1)
        packed = part if packed is None else packed + part
    return packed


def wide_row(main, left, right, r, rows):
    lane = lax.broadcasted_iota(jnp.int32, left.shape, 1)
    if r:
        back = LANES - LANES // rows * r
        left, right = pltpu.roll(left, back, 1), pltpu.roll(right, back, 1)
    side = jnp.where(lane < 2, right, jnp.where(lane >= LANES - 2, left, 0.0))
    return jnp.concatenate([main, side], axis=1)


def three(row, forward):
    width = row.shape[1]
    before, after = pltpu.roll(row, 1, 1), pltpu.roll(row, width - 1, 1)
    parts = [before, row, after] if forward else [after, row, before]
    return jnp.concatenate(parts, axis=0)


def fold_three(stack, forward, columns):
    k = stack.shape[0] // 3
    width = stack.shape[1]
    first, mid, last = stack[:k], stack[k : 2 * k], stack[2 * k :]
    one, other = (1, width - 1) if forward else (width - 1, 1)
    return (pltpu.roll(first, one, 1) + mid + pltpu.roll(last, other, 1))[:, :columns]


def kernel(
    cfg,
    state_hbm, direction_hbm, index_hbm, weight_hbm, mask_hbm,
    air_bias_hbm, air_flux_hbm, react_hbm, sea_bias_hbm, sea_force_hbm,
    aw1_hbm, aw2_hbm, sw1_hbm, sw2_hbm,
    image_ref,
    product_ref,
    raw, wide_raw, index_raw, weight_raw, mask_raw,
    air_bias, air_flux, react_in, sea_bias, sea_force, slim,
    aw1_raw, aw2_raw, sw1_raw, sw2_raw, load,
    aw1, aw1t, aw2, aw2t,
    sw1, sw1t, sw2, sw2t,
    inp,
    edge_a, tiles_a, edges_a,
    cot, edge_b, tiles_b, edges_b,
    pay, paid, out_win, in_win,
    onehot, share_hi, values,
    ax, av, aslope, az,
    sx, sv, sslope, sz,
    send_a, recv_a, send_b, recv_b, send_c, recv_c, send_d, recv_d,
):
    rows, columns, lat_n, lon_n, air_k, air_h, sea_k, sea_h = cfg
    cells = rows * columns
    comp, lat, lon = (lax.axis_index(a) for a in ("comp", "lat", "lon"))
    is_air = comp == 0
    is_sea = comp == 1
    mine = {"comp": comp, "lat": lat, "lon": lon}
    del mine

    def exists(dl):
        return lat + dl >= 0 if dl < 0 else lat + dl < lat_n

    def there(dl, dn):
        return (comp, (lat + dl + lat_n) % lat_n, (lon + dn + lon_n) % lon_n)

    def across(dn):
        return (1 - comp, lat, (lon + dn + lon_n) % lon_n)

    def when(dl, act):
        if dl == 0:
            act()
        else:
            pl.when(exists(dl))(act)

    fetch = [pltpu.make_async_copy(src, dst, load.at[i]) for i, (src, dst) in enumerate((
        (state_hbm, raw.at[0]), (direction_hbm, raw.at[1]),
        (index_hbm, index_raw), (weight_hbm, weight_raw), (mask_hbm, mask_raw),
        (air_bias_hbm, air_bias), (air_flux_hbm, air_flux), (react_hbm, react_in),
        (sea_bias_hbm, sea_bias), (sea_force_hbm, sea_force),
        (aw1_hbm, aw1_raw), (aw2_hbm, aw2_raw), (sw1_hbm, sw1_raw), (sw2_hbm, sw2_raw)))]
    for c in fetch[:10]:
        c.start()

    @pl.when(is_air)
    def _():
        for c in fetch[10:12]:
            c.start()

    @pl.when(is_sea)
    def _():
        for c in fetch[12:14]:
            c.start()

    barrier = pltpu.get_barrier_semaphore()
    for dl, dn in WAYS:
        when(dl, lambda dl=dl, dn=dn: pl.semaphore_signal(
            barrier, inc=1, device_id=there(dl, dn), device_id_type=MESH))
    for dn in (-1, 0, 1):
        pl.semaphore_signal(barrier, inc=1, device_id=across(dn), device_id_type=MESH)

    def halo(tile, edge, tiles, edges, send, recv):
        copies = []
        for i, (dl, dn) in enumerate(WAYS):
            n = i - len(TILE_WAYS)
            copies.append(pltpu.make_async_remote_copy(
                src_ref=tile if n < 0 else edge,
                dst_ref=tiles.at[i] if n < 0 else edges.at[n],
                send_sem=send.at[i], recv_sem=recv.at[i],
                device_id=there(dl, dn), device_id_type=MESH))
        return copies

    def clear(tiles, edges):
        for i, (dl, dn) in enumerate(WAYS):
            n = i - len(TILE_WAYS)

            def act(i=i, n=n):
                if n < 0:
                    tiles[i] = jnp.zeros(tiles.shape[1:], BF16)
                else:
                    edges[n] = jnp.zeros(edges.shape[1:], BF16)

            if dl:
                pl.when(jnp.logical_not(exists(-dl)))(act)

    def start(copies):
        for (dl, dn), c in zip(WAYS, copies):
            when(dl, c.start)

    def wait_recv(copies):
        for (dl, dn), c in zip(WAYS, copies):
            when(-dl, c.wait_recv)

    def wait_send(copies):
        for (dl, dn), c in zip(WAYS, copies):
            when(dl, c.wait_send)

    halo_a = halo(inp, edge_a, tiles_a, edges_a, send_a, recv_a)
    halo_b = halo(cot, edge_b, tiles_b, edges_b, send_b, recv_b)
    pays = [pltpu.make_async_remote_copy(
        src_ref=pay, dst_ref=paid.at[i], send_sem=send_c.at[i], recv_sem=recv_c.at[i],
        device_id=across(dn), device_id_type=MESH) for i, dn in enumerate((0, -1))]
    wins = [pltpu.make_async_remote_copy(
        src_ref=out_win, dst_ref=in_win.at[i], send_sem=send_d.at[i], recv_sem=recv_d.at[i],
        device_id=across(dn), device_id_type=MESH) for i, dn in enumerate((0, 1))]

    for i in range(2):
        fetch[i].wait()
        wide_raw[...] = raw[i].astype(F32)
        channels = raw.shape[1]
        for r in range(rows):
            inp[i * channels : (i + 1) * channels, r * columns : (r + 1) * columns] = (
                wide_raw[:, r, :].astype(BF16))
    edge_a[...] = pack_edges(inp[...].astype(F32), rows, columns).astype(BF16)
    pay[...] = jnp.zeros(pay.shape, F32)

    @pl.when(is_sea)
    def _():
        base = 2 * sea_k
        centre = inp[base : 2 * base, :].astype(F32)
        pay[0:1, :] = centre[0:1]
        pay[1:2, :] = centre[sea_k : sea_k + 1]

    up = jnp.where(exists(-1), 3, 0)
    down = jnp.where(exists(1), 3, 0)
    pl.semaphore_wait(barrier, 5 + up + down)
    start(halo_a)

    @pl.when(is_sea)
    def _():
        for c in pays:
            c.start()

    clear(tiles_a, edges_a)
    clear(tiles_b, edges_b)

    for c in fetch[2:10]:
        c.wait()
    index = jnp.concatenate([index_raw[:, r, :] for r in range(rows)], axis=1)
    weight = jnp.concatenate([weight_raw[:, r, :] for r in range(rows)], axis=1).astype(F32)
    slim[...] = jnp.zeros(slim.shape, F32)
    slim[0:1, 0:air_h] = air_bias[...]
    slim[1:2, 0:sea_h] = sea_bias[...]
    slim[2:4, 0:air_k] = air_flux[...].astype(F32)
    slim[4:5, 0:air_k] = react_in[...]
    slim[5:7, 0:sea_k] = sea_force[...].astype(F32)
    par = jnp.transpose(slim[...])
    share_bias = par[0:air_h, 0:1], par[0:sea_h, 1:2]

    def lay_out(first_raw, second_raw, w1, w1t, w2, w2t):
        hidden, deep = first_raw.shape[2], w1.shape[1] // 3
        blank = jnp.zeros((deep - first_raw.shape[1], hidden), F32)
        for a in range(3):
            back = 2 - a
            tall = lambda ref: jnp.concatenate([ref[a].astype(F32), blank], axis=0)
            w1[:, a * deep : (a + 1) * deep] = jnp.transpose(tall(first_raw)).astype(BF16)
            w2t[:, back * deep : (back + 1) * deep] = jnp.transpose(tall(second_raw)).astype(BF16)
            w1t[:, back * hidden : (back + 1) * hidden] = first_raw[a]
            w2[:, a * hidden : (a + 1) * hidden] = second_raw[a]

    @pl.when(is_air)
    def _():
        for c in fetch[10:12]:
            c.wait()
        lay_out(aw1_raw, aw2_raw, aw1, aw1t, aw2, aw2t)

    @pl.when(is_sea)
    def _():
        for c in fetch[12:14]:
            c.wait()
        lay_out(sw1_raw, sw2_raw, sw1, sw1t, sw2, sw2t)

    near = jnp.sum(weight[0:4], axis=0, keepdims=True)
    far = jnp.sum(weight[4:8], axis=0, keepdims=True)
    slot8 = lax.broadcasted_iota(jnp.int32, weight.shape, 0)
    total = jnp.where(is_air, near + far, jnp.where(slot8 < 4, near, far))
    share = weight / total
    high = lax.shift_right_logical(index, LANES.bit_length() - 1)
    low = index & (LANES - 1)
    place = lax.broadcasted_iota(jnp.int32, (LANES, cells), 0)
    wrows = values.shape[0]
    row16 = lax.broadcasted_iota(jnp.int32, (wrows, cells), 0)
    row16 = jnp.where(is_air, row16, row16 % (wrows // 2))
    for s in range(8):
        onehot[:, s * cells : (s + 1) * cells] = jnp.where(
            place == low[s : s + 1], 1.0, 0.0).astype(BF16)
        share_hi[:, s * cells : (s + 1) * cells] = jnp.where(
            row16 == high[s : s + 1], share[s : s + 1], 0.0)

    per = columns // LANES

    def gather():
        for f in range(2):
            for r in range(rows):
                for nxt in range(2):
                    for h in range(per):
                        at = ((f * rows + r) * 2 + nxt) * per + h
                        lane0 = r * columns + h * LANES
                        values[at : at + 1, :] = paid[nxt, f : f + 1, lane0 : lane0 + LANES]
        got = split_dot(values[...], onehot[...], ((1,), (0,))) * share_hi[...]
        parts = [got[:, s * cells : (s + 1) * cells] for s in range(8)]
        return sum(parts[1:4], parts[0]), sum(parts[5:8], parts[4])

    def scatter(first, second):
        spread = jnp.concatenate([first] * 4 + [second] * 4, axis=1) * share_hi[...]
        out_win[...] = split_dot(spread, onehot[...], ((1,), (1,)))

    def arrived():
        fields = []
        for f in range(2):
            pieces = []
            for r in range(rows):
                for h in range(per):
                    own = ((f * rows + r) * 2) * per + h
                    pieces.append(in_win[0, own : own + 1, :] + in_win[1, own + per : own + per + 1, :])
            fields.append(jnp.concatenate(pieces, axis=1))
        return fields

    def place_of(q, split):
        height = rows * split
        where = -1 if q < 0 else (1 if q >= height else 0)
        q = q - where * height
        return where, q // rows, q % rows

    def stacks(tile, tiles, edges, base, k, split, forward, dst):
        lo, hi = base, base + k * split
        own = tile[lo:hi, :].astype(F32)
        above, below = tiles[1, lo:hi, :].astype(F32), tiles[0, lo:hi, :].astype(F32)
        edge = [edges[n, lo:hi, :].astype(F32) for n in range(6)]
        lefts = {0: edge[1], -1: edge[5], 1: edge[3]}
        rights = {0: edge[0], -1: edge[4], 1: edge[2]}
        mains = {0: own, -1: above, 1: below}
        for p in range(rows * split + 4):
            where, s, r = place_of(p - 2, split)
            ch = slice(s * k, (s + 1) * k)
            row = wide_row(mains[where][ch, r * columns : (r + 1) * columns],
                           lefts[where][ch], rights[where][ch], r, rows)
            dst[p] = jnp.concatenate(
                [three(row, forward), jnp.zeros((dst.shape[1] - 3 * k, row.shape[1]), F32)],
                axis=0).astype(BF16)

    def keep(p, height):
        gone = ((p == 0) & (lat == 0)) | ((p == height + 1) & (lat == lat_n - 1))
        return jnp.where(gone, 0.0, 1.0)

    def rows_of(ref, p):
        return ref[pl.ds(p, 3)].reshape(3 * ref.shape[1], ref.shape[2])

    def give(out, value):
        for r in range(rows):
            wide_raw[:, r, :] = value[:, r * columns : (r + 1) * columns]
        out[...] = wide_raw[...].astype(BF16)

    def first_conv(w1, bias, x, v, slope, z, height):
        def body(p, carry):
            pre = dot(w1[...], rows_of(x, p)) + bias
            t = jnp.tanh(pre)
            s = 1.0 - t * t
            slope[p] = s
            lin = dot(w1[...], rows_of(v, p))
            z[p] = (s * keep(p, height) * lin).astype(BF16)
            return carry
        lax.fori_loop(0, height + 2, body, 0)

    def second_conv(w2, z, height):
        return [fold_three(dot(w2[...], rows_of(z, i)), True, columns) for i in range(height)]

    def second_back(w2t, c, slope, z, height):
        def body(p, carry):
            lin = dot(w2t[...], rows_of(c, p))
            z[p] = (slope[p] * keep(p, height) * lin).astype(BF16)
            return carry
        lax.fori_loop(0, height + 2, body, 0)

    def first_back(w1t, z, height):
        return [fold_three(dot(w1t[...], rows_of(z, i)), False, columns) for i in range(height)]

    def packed(fine, split):
        parts = [jnp.concatenate(fine[s * rows : (s + 1) * rows], axis=1) for s in range(split)]
        return parts

    flux0, flux1 = par[0:air_k, 2:3], par[0:air_k, 3:4]
    react = par[0:air_k, 4:5]
    force0, force1 = par[0:sea_k, 5:6], par[0:sea_k, 6:7]
    half_rows = wrows // 2
    wait_recv(halo_a)

    @pl.when(is_air)
    def _():
        stacks(inp, tiles_a, edges_a, 0, air_k, 1, True, ax)
        stacks(inp, tiles_a, edges_a, air_k, air_k, 1, True, av)
        first_conv(aw1, share_bias[0], ax, av, aslope, az, rows)
        y = packed(second_conv(aw2, az, rows), 1)[0]
        pay[0:1, :] = jnp.sum(flux0 * y, axis=0, keepdims=True)
        pay[1:2, :] = jnp.sum(flux1 * y, axis=0, keepdims=True)
        for c in pays:
            c.start()
        for c in pays:
            c.wait_recv()
        near, far = gather()
        lifted = jnp.sum(near + far, axis=0, keepdims=True)
        image = (y + react * lifted).astype(BF16)
        wide = image.astype(F32)
        give(image_ref, wide)
        surface = jnp.sum(react * wide, axis=0, keepdims=True)
        source = jnp.broadcast_to(surface, (wrows, cells))
        scatter(source, source)
        for c in wins:
            c.start()
        for c in wins:
            c.wait_recv()
        back0, back1 = arrived()
        total = wide + (flux0 * back0 + flux1 * back1)
        cot[...] = total.astype(BF16)
        edge_b[...] = pack_edges(cot[...].astype(F32), rows, columns).astype(BF16)

    @pl.when(is_sea)
    def _():
        stacks(inp, tiles_a, edges_a, 0, sea_k, 2, True, sx)
        stacks(inp, tiles_a, edges_a, 2 * sea_k, sea_k, 2, True, sv)
        first_conv(sw1, share_bias[1], sx, sv, sslope, sz, 2 * rows)
        ys = packed(second_conv(sw2, sz, 2 * rows), 2)
        for c in pays:
            c.wait_recv()
        images, sources = [], []
        row_at = lax.broadcasted_iota(jnp.int32, (wrows, cells), 0)
        for t, got in enumerate(gather()):
            f0 = jnp.sum(got[:half_rows], axis=0, keepdims=True)
            f1 = jnp.sum(got[half_rows:], axis=0, keepdims=True)
            mask = jnp.concatenate(
                [mask_raw[t, r : r + 1, :] for r in range(rows)], axis=1).astype(F32)
            one = (mask * (ys[t] + (force0 * f0 + force1 * f1))).astype(BF16).astype(F32)
            images.append(one)
            pulled0 = jnp.sum(force0 * one, axis=0, keepdims=True)
            pulled1 = jnp.sum(force1 * one, axis=0, keepdims=True)
            sources.append(jnp.where(row_at < half_rows, pulled0, pulled1))
        scatter(*sources)
        for c in wins:
            c.start()
        image = jnp.concatenate(images, axis=0).astype(BF16)
        cot[...] = image
        edge_b[...] = pack_edges(image.astype(F32), rows, columns).astype(BF16)

    start(halo_b)

    @pl.when(is_sea)
    def _():
        give(image_ref, cot[...].astype(F32))

    wait_recv(halo_b)

    @pl.when(is_air)
    def _():
        stacks(cot, tiles_b, edges_b, 0, air_k, 1, False, ax)
        second_back(aw2t, ax, aslope, az, rows)
        give(product_ref, packed(first_back(aw1t, az, rows), 1)[0])

    @pl.when(is_sea)
    def _():
        stacks(cot, tiles_b, edges_b, 0, sea_k, 2, False, sx)
        second_back(sw2t, sx, sslope, sz, 2 * rows)
        fine = packed(first_back(sw1t, sz, 2 * rows), 2)
        for c in wins:
            c.wait_recv()
        top = lax.broadcasted_iota(jnp.int32, (sea_k, cells), 0) == 0
        fine = [f + jnp.where(top, b, 0.0) for f, b in zip(fine, arrived())]
        give(product_ref, jnp.concatenate(fine, axis=0))

    for c in pays + wins:
        c.wait_send()
    wait_send(halo_a)
    wait_send(halo_b)


def shards(
    lat_n, lon_n, state, direction, air_first, air_bias, air_second, air_flux, reaction,
    sea_first, sea_bias, sea_second, sea_forcing, regrid_index, regrid_weight, land_mask,
):
    channels, rows, columns = state.shape[1:]
    cells = rows * columns
    air_h, air_k = air_first.shape[1:]
    sea_h, sea_k = sea_first.shape[1:]
    def rowed(w):
        return w.reshape(3, 3 * w.shape[1], w.shape[2])

    args = [
        state[0], direction[0], regrid_index[0], regrid_weight[0], land_mask,
        air_bias[None], air_flux, reaction[None], sea_bias[None], sea_forcing.T,
        rowed(air_first.transpose(0, 2, 1)), rowed(air_second),
        rowed(sea_first.transpose(0, 2, 1)), rowed(sea_second),
    ]
    air_deep, sea_deep = 3 * air_k + -3 * air_k % LANES, 3 * sea_k + -3 * sea_k % LANES
    tall = max(air_h, sea_h)
    wide = columns + LANES
    wrows = 2 * rows * 2 * columns // LANES
    dma = pltpu.SemaphoreType.DMA
    vmem = pltpu.VMEM
    image, product = pl.pallas_call(
        functools.partial(kernel, (rows, columns, lat_n, lon_n, air_k, air_h, sea_k, sea_h)),
        out_shape=[jax.ShapeDtypeStruct((channels, rows, columns), BF16)] * 2,
        in_specs=[pl.BlockSpec(memory_space=pl.ANY)] * len(args),
        out_specs=[pl.BlockSpec(memory_space=pltpu.VMEM)] * 2,
        scratch_shapes=[
            vmem((2, channels, rows, columns), BF16),
            vmem((channels, rows, columns), F32),
            vmem(args[2].shape, jnp.int32),
            vmem(args[3].shape, jnp.int32),
            vmem(args[4].shape, jnp.int32),
            *[vmem(a.shape, a.dtype) for a in args[5:10]],
            vmem((LANES, tall), F32),
            *[vmem(a.shape, a.dtype) for a in args[10:14]],
            dma((14,)),
            vmem((air_h, 3 * air_deep), BF16),
            vmem((3 * air_k, 3 * air_h), BF16),
            vmem((3 * air_k, 3 * air_h), BF16),
            vmem((air_h, 3 * air_deep), BF16),
            vmem((sea_h, 3 * sea_deep), BF16),
            vmem((3 * sea_k, 3 * sea_h), BF16),
            vmem((3 * sea_k, 3 * sea_h), BF16),
            vmem((sea_h, 3 * sea_deep), BF16),
            vmem((2 * channels, cells), BF16),
            vmem((2 * channels, LANES), BF16),
            vmem((2, 2 * channels, cells), BF16),
            vmem((6, 2 * channels, LANES), BF16),
            vmem((channels, cells), BF16),
            vmem((channels, LANES), BF16),
            vmem((2, channels, cells), BF16),
            vmem((6, channels, LANES), BF16),
            vmem((8, cells), F32),
            vmem((2, 8, cells), F32),
            vmem((wrows, LANES), F32),
            vmem((2, wrows, LANES), F32),
            vmem((LANES, 8 * cells), BF16),
            vmem((wrows, 8 * cells), F32),
            vmem((wrows, LANES), F32),
            vmem((rows + 4, air_deep, wide), BF16),
            vmem((rows + 4, air_deep, wide), BF16),
            vmem((rows + 2, air_h, wide), F32),
            vmem((rows + 2, air_h, wide), BF16),
            vmem((2 * rows + 4, sea_deep, wide), BF16),
            vmem((2 * rows + 4, sea_deep, wide), BF16),
            vmem((2 * rows + 2, sea_h, wide), F32),
            vmem((2 * rows + 2, sea_h, wide), BF16),
            dma((8,)), dma((8,)), dma((8,)), dma((8,)), dma((2,)), dma((2,)), dma((2,)), dma((2,)),
        ],
        compiler_params=pltpu.CompilerParams(
            collective_id=0, has_side_effects=True, vmem_limit_bytes=48 * 1024 * 1024),
        name="coupled",
    )(*args)
    return image[None], product[None]


def solution(mesh):
    field = P("comp", None, "lat", "lon")
    return jax.shard_map(
        functools.partial(shards, mesh.shape["lat"], mesh.shape["lon"]),
        mesh=mesh,
        in_specs=(field, field) + (P(),) * 9 + (field, field, P(None, "lat", "lon")),
        out_specs=(field, field),
        check_vma=False,
    )
```

```python
import functools

import jax
import jax.numpy as jnp
from jax import lax
from jax.experimental import pallas as pl
from jax.experimental.pallas import tpu as pltpu
from jax.sharding import PartitionSpec as P

MESH = pl.DeviceIdType.MESH
F32 = jnp.float32
BF16 = jnp.bfloat16
LANES = 128
LINES = 16
TILE_WAYS = ((-1, 0), (1, 0))
EDGE_WAYS = ((0, -1), (0, 1), (-1, -1), (-1, 1), (1, -1), (1, 1))
WAYS = TILE_WAYS + EDGE_WAYS


def dot(a, b):
    return jnp.dot(a, b, preferred_element_type=F32)


def split_dot(a, b, dims):
    high = a.astype(BF16)
    low = (a - high.astype(F32)).astype(BF16)
    both = lax.dot_general(
        jnp.concatenate([high, low], axis=0), b, (dims, ((), ())), preferred_element_type=F32
    )
    return both[: a.shape[0]] + both[a.shape[0] :]


def pack_edges(tile, rows, columns):
    channels = tile.shape[0]
    lane = lax.broadcasted_iota(jnp.int32, (channels, LANES), 1)
    packed = None
    for r in range(rows):
        first = tile[:, r * columns : r * columns + LANES]
        last = tile[:, (r + 1) * columns - LANES : (r + 1) * columns]
        part = jnp.where(lane < 2, first, jnp.where(lane >= LANES - 2, last, 0.0))
        part = pltpu.roll(part, 2 + 4 * r, 1)
        packed = part if packed is None else packed + part
    blank = jnp.zeros((-channels % LANES, LANES), F32)
    return jnp.transpose(jnp.concatenate([packed, blank], axis=0))[:LINES].astype(BF16)


def unpack_edges(edges):
    lines = [edges[n].astype(F32) for n in range(len(EDGE_WAYS))]
    blank = jnp.zeros((LANES - LINES * len(lines), lines[0].shape[1]), F32)
    return jnp.transpose(jnp.concatenate(lines + [blank], axis=0))


def wide_row(main, sides, left, right, r):
    lane = lax.broadcasted_iota(jnp.int32, sides.shape, 1)
    before = pltpu.roll(sides, (LANES - 2 - LINES * left - 4 * r) % LANES, 1)
    after = pltpu.roll(sides, -(LINES * right + 4 * r + 2) % LANES, 1)
    side = jnp.where(lane < 2, after, jnp.where(lane >= LANES - 2, before, 0.0))
    return jnp.concatenate([main, side], axis=1)


def three(row, forward):
    width = row.shape[1]
    before, after = pltpu.roll(row, 1, 1), pltpu.roll(row, width - 1, 1)
    parts = [before, row, after] if forward else [after, row, before]
    return jnp.concatenate(parts, axis=0)


def fold_three(stack, forward, columns):
    k = stack.shape[0] // 3
    width = stack.shape[1]
    first, mid, last = stack[:k], stack[k : 2 * k], stack[2 * k :]
    one, other = (1, width - 1) if forward else (width - 1, 1)
    return (pltpu.roll(first, one, 1) + mid + pltpu.roll(last, other, 1))[:, :columns]


def kernel(
    cfg,
    state_hbm, direction_hbm, index_hbm, weight_hbm, mask_hbm,
    air_bias_hbm, air_flux_hbm, react_hbm, sea_bias_hbm, sea_force_hbm,
    aw1_hbm, aw2_hbm, sw1_hbm, sw2_hbm,
    image_ref,
    product_ref,
    raw, wide_raw, index_raw, weight_raw, mask_raw,
    air_bias, air_flux, react_in, sea_bias, sea_force, slim,
    aw1_raw, aw2_raw, sw1_raw, sw2_raw, load,
    aw1, aw1t, aw2, aw2t,
    sw1, sw1t, sw2, sw2t,
    inp,
    edge_a, tiles_a, edges_a,
    cot, edge_b, tiles_b, edges_b,
    pay, paid, out_win, in_win,
    onehot, share_hi, values,
    ax, av, aslope, az,
    sx, sv, sslope, sz,
    send_a, recv_a, send_b, recv_b, send_c, recv_c, send_d, recv_d,
):
    rows, columns, lat_n, lon_n, air_k, air_h, sea_k, sea_h = cfg
    cells = rows * columns
    comp, lat, lon = (lax.axis_index(a) for a in ("comp", "lat", "lon"))
    is_air = comp == 0
    is_sea = comp == 1
    mine = {"comp": comp, "lat": lat, "lon": lon}
    del mine

    def exists(dl):
        return lat + dl >= 0 if dl < 0 else lat + dl < lat_n

    def there(dl, dn):
        return (comp, (lat + dl + lat_n) % lat_n, (lon + dn + lon_n) % lon_n)

    def across(dn):
        return (1 - comp, lat, (lon + dn + lon_n) % lon_n)

    def when(dl, act):
        if dl == 0:
            act()
        else:
            pl.when(exists(dl))(act)

    fetch = [pltpu.make_async_copy(src, dst, load.at[i]) for i, (src, dst) in enumerate((
        (state_hbm, raw.at[0]), (direction_hbm, raw.at[1]),
        (index_hbm, index_raw), (weight_hbm, weight_raw), (mask_hbm, mask_raw),
        (air_bias_hbm, air_bias), (air_flux_hbm, air_flux), (react_hbm, react_in),
        (sea_bias_hbm, sea_bias), (sea_force_hbm, sea_force),
        (aw1_hbm, aw1_raw), (aw2_hbm, aw2_raw), (sw1_hbm, sw1_raw), (sw2_hbm, sw2_raw)))]
    for c in fetch[:10]:
        c.start()

    @pl.when(is_air)
    def _():
        for c in fetch[10:12]:
            c.start()

    @pl.when(is_sea)
    def _():
        for c in fetch[12:14]:
            c.start()

    barrier = pltpu.get_barrier_semaphore()
    for dl, dn in WAYS:
        when(dl, lambda dl=dl, dn=dn: pl.semaphore_signal(
            barrier, inc=1, device_id=there(dl, dn), device_id_type=MESH))
    for dn in (-1, 0, 1):
        pl.semaphore_signal(barrier, inc=1, device_id=across(dn), device_id_type=MESH)

    def halo(tile, edge, tiles, edges, send, recv):
        copies = []
        for i, (dl, dn) in enumerate(WAYS):
            n = i - len(TILE_WAYS)
            copies.append(pltpu.make_async_remote_copy(
                src_ref=tile if n < 0 else edge,
                dst_ref=tiles.at[i] if n < 0 else edges.at[n],
                send_sem=send.at[i], recv_sem=recv.at[i],
                device_id=there(dl, dn), device_id_type=MESH))
        return copies

    def clear(tiles, edges):
        for i, (dl, dn) in enumerate(WAYS):
            n = i - len(TILE_WAYS)

            def act(i=i, n=n):
                if n < 0:
                    tiles[i] = jnp.zeros(tiles.shape[1:], BF16)
                else:
                    edges[n] = jnp.zeros(edges.shape[1:], BF16)

            if dl:
                pl.when(jnp.logical_not(exists(-dl)))(act)

    def start(copies, ways=WAYS):
        for way, c in zip(WAYS, copies):
            if way in ways:
                when(way[0], c.start)

    def wait_recv(copies):
        for (dl, dn), c in zip(WAYS, copies):
            when(-dl, c.wait_recv)

    def wait_send(copies):
        for (dl, dn), c in zip(WAYS, copies):
            when(dl, c.wait_send)

    halo_a = halo(inp, edge_a, tiles_a, edges_a, send_a, recv_a)
    halo_b = halo(cot, edge_b, tiles_b, edges_b, send_b, recv_b)
    pays = [pltpu.make_async_remote_copy(
        src_ref=pay, dst_ref=paid.at[i], send_sem=send_c.at[i], recv_sem=recv_c.at[i],
        device_id=across(dn), device_id_type=MESH) for i, dn in enumerate((0, -1))]
    wins = [pltpu.make_async_remote_copy(
        src_ref=out_win, dst_ref=in_win.at[i], send_sem=send_d.at[i], recv_sem=recv_d.at[i],
        device_id=across(dn), device_id_type=MESH) for i, dn in enumerate((0, 1))]

    for i in range(2):
        fetch[i].wait()
        wide_raw[...] = raw[i].astype(F32)
        channels = raw.shape[1]
        for r in range(rows):
            inp[i * channels : (i + 1) * channels, r * columns : (r + 1) * columns] = (
                wide_raw[:, r, :].astype(BF16))
    pay[...] = jnp.zeros(pay.shape, F32)

    @pl.when(is_sea)
    def _():
        base = 2 * sea_k
        centre = inp[base : 2 * base, :].astype(F32)
        pay[0:1, :] = centre[0:1]
        pay[1:2, :] = centre[sea_k : sea_k + 1]

    up = jnp.where(exists(-1), 3, 0)
    down = jnp.where(exists(1), 3, 0)
    pl.semaphore_wait(barrier, 5 + up + down)
    start(halo_a, TILE_WAYS)
    edge_a[...] = pack_edges(inp[...].astype(F32), rows, columns)
    start(halo_a, EDGE_WAYS)

    @pl.when(is_sea)
    def _():
        for c in pays:
            c.start()

    clear(tiles_a, edges_a)
    clear(tiles_b, edges_b)

    for c in fetch[2:10]:
        c.wait()
    index = jnp.concatenate([index_raw[:, r, :] for r in range(rows)], axis=1)
    weight = jnp.concatenate([weight_raw[:, r, :] for r in range(rows)], axis=1).astype(F32)
    slim[...] = jnp.zeros(slim.shape, F32)
    slim[0:1, 0:air_h] = air_bias[...]
    slim[1:2, 0:sea_h] = sea_bias[...]
    slim[2:4, 0:air_k] = air_flux[...].astype(F32)
    slim[4:5, 0:air_k] = react_in[...]
    slim[5:7, 0:sea_k] = sea_force[...].astype(F32)
    par = jnp.transpose(slim[...])
    share_bias = par[0:air_h, 0:1], par[0:sea_h, 1:2]

    def lay_out(first_raw, second_raw, w1, w1t, w2, w2t):
        hidden, deep = first_raw.shape[2], w1.shape[1] // 3
        blank = jnp.zeros((deep - first_raw.shape[1], hidden), F32)
        for a in range(3):
            back = 2 - a
            tall = lambda ref: jnp.concatenate([ref[a].astype(F32), blank], axis=0)
            w1[:, a * deep : (a + 1) * deep] = jnp.transpose(tall(first_raw)).astype(BF16)
            w2t[:, back * deep : (back + 1) * deep] = jnp.transpose(tall(second_raw)).astype(BF16)
            w1t[:, back * hidden : (back + 1) * hidden] = first_raw[a]
            w2[:, a * hidden : (a + 1) * hidden] = second_raw[a]

    @pl.when(is_air)
    def _():
        for c in fetch[10:12]:
            c.wait()
        lay_out(aw1_raw, aw2_raw, aw1, aw1t, aw2, aw2t)

    @pl.when(is_sea)
    def _():
        for c in fetch[12:14]:
            c.wait()
        lay_out(sw1_raw, sw2_raw, sw1, sw1t, sw2, sw2t)

    near = jnp.sum(weight[0:4], axis=0, keepdims=True)
    far = jnp.sum(weight[4:8], axis=0, keepdims=True)
    slot8 = lax.broadcasted_iota(jnp.int32, weight.shape, 0)
    total = jnp.where(is_air, near + far, jnp.where(slot8 < 4, near, far))
    share = weight / total
    high = lax.shift_right_logical(index, LANES.bit_length() - 1)
    low = index & (LANES - 1)
    place = lax.broadcasted_iota(jnp.int32, (LANES, cells), 0)
    wrows = values.shape[0]
    row16 = lax.broadcasted_iota(jnp.int32, (wrows, cells), 0)
    row16 = jnp.where(is_air, row16, row16 % (wrows // 2))
    for s in range(8):
        onehot[:, s * cells : (s + 1) * cells] = jnp.where(
            place == low[s : s + 1], 1.0, 0.0).astype(BF16)
        share_hi[:, s * cells : (s + 1) * cells] = jnp.where(
            row16 == high[s : s + 1], share[s : s + 1], 0.0)

    per = columns // LANES

    def gather():
        for f in range(2):
            for r in range(rows):
                for nxt in range(2):
                    for h in range(per):
                        at = ((f * rows + r) * 2 + nxt) * per + h
                        lane0 = r * columns + h * LANES
                        values[at : at + 1, :] = paid[nxt, f : f + 1, lane0 : lane0 + LANES]
        got = split_dot(values[...], onehot[...], ((1,), (0,))) * share_hi[...]
        parts = [got[:, s * cells : (s + 1) * cells] for s in range(8)]
        return sum(parts[1:4], parts[0]), sum(parts[5:8], parts[4])

    def scatter(first, second):
        spread = jnp.concatenate([first] * 4 + [second] * 4, axis=1) * share_hi[...]
        out_win[...] = split_dot(spread, onehot[...], ((1,), (1,)))

    def arrived():
        fields = []
        for f in range(2):
            pieces = []
            for r in range(rows):
                for h in range(per):
                    own = ((f * rows + r) * 2) * per + h
                    pieces.append(in_win[0, own : own + 1, :] + in_win[1, own + per : own + per + 1, :])
            fields.append(jnp.concatenate(pieces, axis=1))
        return fields

    def place_of(q, split):
        height = rows * split
        where = -1 if q < 0 else (1 if q >= height else 0)
        q = q - where * height
        return where, q // rows, q % rows

    def stacks(tile, tiles, edges, base, k, split, forward, dst):
        lo, hi = base, base + k * split
        own = tile[lo:hi, :].astype(F32)
        above, below = tiles[1, lo:hi, :].astype(F32), tiles[0, lo:hi, :].astype(F32)
        sides = unpack_edges(edges)[lo:hi]
        lefts = {0: 1, -1: 5, 1: 3}
        rights = {0: 0, -1: 4, 1: 2}
        mains = {0: own, -1: above, 1: below}
        for p in range(rows * split + 4):
            where, s, r = place_of(p - 2, split)
            ch = slice(s * k, (s + 1) * k)
            row = wide_row(mains[where][ch, r * columns : (r + 1) * columns],
                           sides[ch], lefts[where], rights[where], r)
            dst[p] = jnp.concatenate(
                [three(row, forward), jnp.zeros((dst.shape[1] - 3 * k, row.shape[1]), F32)],
                axis=0).astype(BF16)

    def keep(p, height):
        gone = ((p == 0) & (lat == 0)) | ((p == height + 1) & (lat == lat_n - 1))
        return jnp.where(gone, 0.0, 1.0)

    def rows_of(ref, p):
        return ref[pl.ds(p, 3)].reshape(3 * ref.shape[1], ref.shape[2])

    def give(out, value):
        for r in range(rows):
            wide_raw[:, r, :] = value[:, r * columns : (r + 1) * columns]
        out[...] = wide_raw[...].astype(BF16)

    def first_conv(w1, bias, x, v, slope, z, height):
        def body(p, carry):
            pre = dot(w1[...], rows_of(x, p)) + bias
            t = jnp.tanh(pre)
            s = 1.0 - t * t
            slope[p] = s
            lin = dot(w1[...], rows_of(v, p))
            z[p] = (s * keep(p, height) * lin).astype(BF16)
            return carry
        lax.fori_loop(0, height + 2, body, 0)

    def second_conv(w2, z, height):
        return [fold_three(dot(w2[...], rows_of(z, i)), True, columns) for i in range(height)]

    def second_back(w2t, c, slope, z, height):
        def body(p, carry):
            lin = dot(w2t[...], rows_of(c, p))
            z[p] = (slope[p] * keep(p, height) * lin).astype(BF16)
            return carry
        lax.fori_loop(0, height + 2, body, 0)

    def first_back(w1t, z, height):
        return [fold_three(dot(w1t[...], rows_of(z, i)), False, columns) for i in range(height)]

    def packed(fine, split):
        parts = [jnp.concatenate(fine[s * rows : (s + 1) * rows], axis=1) for s in range(split)]
        return parts

    flux0, flux1 = par[0:air_k, 2:3], par[0:air_k, 3:4]
    react = par[0:air_k, 4:5]
    force0, force1 = par[0:sea_k, 5:6], par[0:sea_k, 6:7]
    half_rows = wrows // 2
    wait_recv(halo_a)

    @pl.when(is_air)
    def _():
        stacks(inp, tiles_a, edges_a, 0, air_k, 1, True, ax)
        stacks(inp, tiles_a, edges_a, air_k, air_k, 1, True, av)
        first_conv(aw1, share_bias[0], ax, av, aslope, az, rows)
        y = packed(second_conv(aw2, az, rows), 1)[0]
        pay[0:1, :] = jnp.sum(flux0 * y, axis=0, keepdims=True)
        pay[1:2, :] = jnp.sum(flux1 * y, axis=0, keepdims=True)
        for c in pays:
            c.start()
        for c in pays:
            c.wait_recv()
        near, far = gather()
        lifted = jnp.sum(near + far, axis=0, keepdims=True)
        image = (y + react * lifted).astype(BF16)
        wide = image.astype(F32)
        give(image_ref, wide)
        surface = jnp.sum(react * wide, axis=0, keepdims=True)
        source = jnp.broadcast_to(surface, (wrows, cells))
        scatter(source, source)
        for c in wins:
            c.start()
        for c in wins:
            c.wait_recv()
        back0, back1 = arrived()
        total = wide + (flux0 * back0 + flux1 * back1)
        cot[...] = total.astype(BF16)
        edge_b[...] = pack_edges(cot[...].astype(F32), rows, columns)

    @pl.when(is_sea)
    def _():
        stacks(inp, tiles_a, edges_a, 0, sea_k, 2, True, sx)
        stacks(inp, tiles_a, edges_a, 2 * sea_k, sea_k, 2, True, sv)
        first_conv(sw1, share_bias[1], sx, sv, sslope, sz, 2 * rows)
        ys = packed(second_conv(sw2, sz, 2 * rows), 2)
        for c in pays:
            c.wait_recv()
        images, sources = [], []
        row_at = lax.broadcasted_iota(jnp.int32, (wrows, cells), 0)
        for t, got in enumerate(gather()):
            f0 = jnp.sum(got[:half_rows], axis=0, keepdims=True)
            f1 = jnp.sum(got[half_rows:], axis=0, keepdims=True)
            mask = jnp.concatenate(
                [mask_raw[t, r : r + 1, :] for r in range(rows)], axis=1).astype(F32)
            one = (mask * (ys[t] + (force0 * f0 + force1 * f1))).astype(BF16).astype(F32)
            images.append(one)
            pulled0 = jnp.sum(force0 * one, axis=0, keepdims=True)
            pulled1 = jnp.sum(force1 * one, axis=0, keepdims=True)
            sources.append(jnp.where(row_at < half_rows, pulled0, pulled1))
        scatter(*sources)
        for c in wins:
            c.start()
        image = jnp.concatenate(images, axis=0).astype(BF16)
        cot[...] = image
        edge_b[...] = pack_edges(image.astype(F32), rows, columns)

    start(halo_b)

    @pl.when(is_sea)
    def _():
        give(image_ref, cot[...].astype(F32))

    wait_recv(halo_b)

    @pl.when(is_air)
    def _():
        stacks(cot, tiles_b, edges_b, 0, air_k, 1, False, ax)
        second_back(aw2t, ax, aslope, az, rows)
        give(product_ref, packed(first_back(aw1t, az, rows), 1)[0])

    @pl.when(is_sea)
    def _():
        stacks(cot, tiles_b, edges_b, 0, sea_k, 2, False, sx)
        second_back(sw2t, sx, sslope, sz, 2 * rows)
        fine = packed(first_back(sw1t, sz, 2 * rows), 2)
        for c in wins:
            c.wait_recv()
        top = lax.broadcasted_iota(jnp.int32, (sea_k, cells), 0) == 0
        fine = [f + jnp.where(top, b, 0.0) for f, b in zip(fine, arrived())]
        give(product_ref, jnp.concatenate(fine, axis=0))

    for c in pays + wins:
        c.wait_send()
    wait_send(halo_a)
    wait_send(halo_b)


def shards(
    lat_n, lon_n, state, direction, air_first, air_bias, air_second, air_flux, reaction,
    sea_first, sea_bias, sea_second, sea_forcing, regrid_index, regrid_weight, land_mask,
):
    channels, rows, columns = state.shape[1:]
    cells = rows * columns
    air_h, air_k = air_first.shape[1:]
    sea_h, sea_k = sea_first.shape[1:]
    def rowed(w):
        return w.reshape(3, 3 * w.shape[1], w.shape[2])

    args = [
        state[0], direction[0], regrid_index[0], regrid_weight[0], land_mask,
        air_bias[None], air_flux, reaction[None], sea_bias[None], sea_forcing.T,
        rowed(air_first.transpose(0, 2, 1)), rowed(air_second),
        rowed(sea_first.transpose(0, 2, 1)), rowed(sea_second),
    ]
    air_deep, sea_deep = 3 * air_k + -3 * air_k % LANES, 3 * sea_k + -3 * sea_k % LANES
    tall = max(air_h, sea_h)
    line_a, line_b = 2 * channels + -2 * channels % LANES, channels + -channels % LANES
    wide = columns + LANES
    wrows = 2 * rows * 2 * columns // LANES
    dma = pltpu.SemaphoreType.DMA
    vmem = pltpu.VMEM
    image, product = pl.pallas_call(
        functools.partial(kernel, (rows, columns, lat_n, lon_n, air_k, air_h, sea_k, sea_h)),
        out_shape=[jax.ShapeDtypeStruct((channels, rows, columns), BF16)] * 2,
        in_specs=[pl.BlockSpec(memory_space=pltpu.HBM)] * len(args),
        out_specs=[pl.BlockSpec(memory_space=pltpu.VMEM)] * 2,
        scratch_shapes=[
            vmem((2, channels, rows, columns), BF16),
            vmem((channels, rows, columns), F32),
            vmem(args[2].shape, jnp.int32),
            vmem(args[3].shape, jnp.int32),
            vmem(args[4].shape, jnp.int32),
            *[vmem(a.shape, a.dtype) for a in args[5:10]],
            vmem((LANES, tall), F32),
            *[vmem(a.shape, a.dtype) for a in args[10:14]],
            dma((14,)),
            vmem((air_h, 3 * air_deep), BF16),
            vmem((3 * air_k, 3 * air_h), BF16),
            vmem((3 * air_k, 3 * air_h), BF16),
            vmem((air_h, 3 * air_deep), BF16),
            vmem((sea_h, 3 * sea_deep), BF16),
            vmem((3 * sea_k, 3 * sea_h), BF16),
            vmem((3 * sea_k, 3 * sea_h), BF16),
            vmem((sea_h, 3 * sea_deep), BF16),
            vmem((2 * channels, cells), BF16),
            vmem((LINES, line_a), BF16),
            vmem((2, 2 * channels, cells), BF16),
            vmem((6, LINES, line_a), BF16),
            vmem((channels, cells), BF16),
            vmem((LINES, line_b), BF16),
            vmem((2, channels, cells), BF16),
            vmem((6, LINES, line_b), BF16),
            vmem((8, cells), F32),
            vmem((2, 8, cells), F32),
            vmem((wrows, LANES), F32),
            vmem((2, wrows, LANES), F32),
            vmem((LANES, 8 * cells), BF16),
            vmem((wrows, 8 * cells), F32),
            vmem((wrows, LANES), F32),
            vmem((rows + 4, air_deep, wide), BF16),
            vmem((rows + 4, air_deep, wide), BF16),
            vmem((rows + 2, air_h, wide), F32),
            vmem((rows + 2, air_h, wide), BF16),
            vmem((2 * rows + 4, sea_deep, wide), BF16),
            vmem((2 * rows + 4, sea_deep, wide), BF16),
            vmem((2 * rows + 2, sea_h, wide), F32),
            vmem((2 * rows + 2, sea_h, wide), BF16),
            dma((8,)), dma((8,)), dma((8,)), dma((8,)), dma((2,)), dma((2,)), dma((2,)), dma((2,)),
        ],
        compiler_params=pltpu.CompilerParams(
            collective_id=0, has_side_effects=True, vmem_limit_bytes=62 * 1024 * 1024),
        name="coupled",
    )(*args)
    return image[None], product[None]


def solution(mesh):
    field = P("comp", None, "lat", "lon")
    return jax.shard_map(
        functools.partial(shards, mesh.shape["lat"], mesh.shape["lon"]),
        mesh=mesh,
        in_specs=(field, field) + (P(),) * 9 + (field, field, P(None, "lat", "lon")),
        out_specs=(field, field),
        check_vma=False,
    )
```

```python
import functools

import jax
import jax.numpy as jnp
from jax import lax
from jax.experimental import pallas as pl
from jax.experimental.pallas import tpu as pltpu
from jax.sharding import PartitionSpec as P

MESH = pl.DeviceIdType.MESH
F32 = jnp.float32
BF16 = jnp.bfloat16
LANES = 128
LINES = 16
TILE_WAYS = ((-1, 0), (1, 0))
EDGE_WAYS = ((0, -1), (0, 1), (-1, -1), (-1, 1), (1, -1), (1, 1))
WAYS = TILE_WAYS + EDGE_WAYS


def dot(a, b):
    return jnp.dot(a, b, preferred_element_type=F32)


def split_dot(a, b, dims):
    high = a.astype(BF16)
    low = (a - high.astype(F32)).astype(BF16)
    both = lax.dot_general(
        jnp.concatenate([high, low], axis=0), b, (dims, ((), ())), preferred_element_type=F32
    )
    return both[: a.shape[0]] + both[a.shape[0] :]


def pack_edges(tile, rows, columns):
    channels = tile.shape[0]
    lane = lax.broadcasted_iota(jnp.int32, (channels, LANES), 1)
    packed = None
    for r in range(rows):
        first = tile[:, r * columns : r * columns + LANES]
        last = tile[:, (r + 1) * columns - LANES : (r + 1) * columns]
        part = jnp.where(lane < 2, first, jnp.where(lane >= LANES - 2, last, 0.0))
        part = pltpu.roll(part, 2 + 4 * r, 1)
        packed = part if packed is None else packed + part
    blank = jnp.zeros((-channels % LANES, LANES), F32)
    return jnp.transpose(jnp.concatenate([packed, blank], axis=0))[:LINES].astype(BF16)


def unpack_edges(edges):
    lines = [edges[n].astype(F32) for n in range(len(EDGE_WAYS))]
    blank = jnp.zeros((LANES - LINES * len(lines), lines[0].shape[1]), F32)
    return jnp.transpose(jnp.concatenate(lines + [blank], axis=0))


def wide_row(main, sides, left, right, r):
    lane = lax.broadcasted_iota(jnp.int32, sides.shape, 1)
    before = pltpu.roll(sides, (LANES - 2 - LINES * left - 4 * r) % LANES, 1)
    after = pltpu.roll(sides, -(LINES * right + 4 * r + 2) % LANES, 1)
    side = jnp.where(lane < 2, after, jnp.where(lane >= LANES - 2, before, 0.0))
    return jnp.concatenate([main, side], axis=1)


def three(row, forward):
    width = row.shape[1]
    before, after = pltpu.roll(row, 1, 1), pltpu.roll(row, width - 1, 1)
    parts = [before, row, after] if forward else [after, row, before]
    return jnp.concatenate(parts, axis=0)


def fold_three(stack, forward, columns):
    k = stack.shape[0] // 3
    width = stack.shape[1]
    first, mid, last = stack[:k], stack[k : 2 * k], stack[2 * k :]
    one, other = (1, width - 1) if forward else (width - 1, 1)
    return (pltpu.roll(first, one, 1) + mid + pltpu.roll(last, other, 1))[:, :columns]


def kernel(
    cfg,
    state_hbm, direction_hbm, index_hbm, weight_hbm, mask_hbm,
    air_bias_hbm, air_flux_hbm, react_hbm, sea_bias_hbm, sea_force_hbm,
    aw1_hbm, aw2_hbm, sw1_hbm, sw2_hbm,
    image_ref,
    product_ref,
    raw, wide_raw, index_raw, weight_raw, mask_raw,
    air_bias, air_flux, react_in, sea_bias, sea_force, slim,
    aw1_raw, aw2_raw, sw1_raw, sw2_raw, load,
    aw1, aw1t, aw2, aw2t,
    sw1, sw1t, sw2, sw2t,
    inp,
    edge_a, tiles_a, edges_a,
    cot, edge_b, tiles_b, edges_b,
    pay, paid, out_win, in_win,
    onehot, share_hi, values,
    ax, av, aslope, az,
    sx, sv, sslope, sz,
    send_a, recv_a, send_b, recv_b, send_c, recv_c, send_d, recv_d,
):
    rows, columns, lat_n, lon_n, air_k, air_h, sea_k, sea_h = cfg
    cells = rows * columns
    comp, lat, lon = (lax.axis_index(a) for a in ("comp", "lat", "lon"))
    is_air = comp == 0
    is_sea = comp == 1
    mine = {"comp": comp, "lat": lat, "lon": lon}
    del mine

    def exists(dl):
        return lat + dl >= 0 if dl < 0 else lat + dl < lat_n

    def there(dl, dn):
        return (comp, (lat + dl + lat_n) % lat_n, (lon + dn + lon_n) % lon_n)

    def across(dn):
        return (1 - comp, lat, (lon + dn + lon_n) % lon_n)

    def when(dl, act):
        if dl == 0:
            act()
        else:
            pl.when(exists(dl))(act)

    fetch = [pltpu.make_async_copy(src, dst, load.at[i]) for i, (src, dst) in enumerate((
        (state_hbm, raw.at[0]), (direction_hbm, raw.at[1]),
        (index_hbm, index_raw), (weight_hbm, weight_raw), (mask_hbm, mask_raw),
        (air_bias_hbm, air_bias), (air_flux_hbm, air_flux), (react_hbm, react_in),
        (sea_bias_hbm, sea_bias), (sea_force_hbm, sea_force),
        (aw1_hbm, aw1_raw), (aw2_hbm, aw2_raw), (sw1_hbm, sw1_raw), (sw2_hbm, sw2_raw)))]
    for c in fetch[:10]:
        c.start()

    @pl.when(is_air)
    def _():
        for c in fetch[10:12]:
            c.start()

    @pl.when(is_sea)
    def _():
        for c in fetch[12:14]:
            c.start()

    barrier = pltpu.get_barrier_semaphore()
    for dl, dn in WAYS:
        when(dl, lambda dl=dl, dn=dn: pl.semaphore_signal(
            barrier, inc=1, device_id=there(dl, dn), device_id_type=MESH))
    for dn in (-1, 0, 1):
        pl.semaphore_signal(barrier, inc=1, device_id=across(dn), device_id_type=MESH)

    def halo(tile, edge, tiles, edges, send, recv):
        copies = []
        for i, (dl, dn) in enumerate(WAYS):
            n = i - len(TILE_WAYS)
            copies.append(pltpu.make_async_remote_copy(
                src_ref=tile if n < 0 else edge,
                dst_ref=tiles.at[i] if n < 0 else edges.at[n],
                send_sem=send.at[i], recv_sem=recv.at[i],
                device_id=there(dl, dn), device_id_type=MESH))
        return copies

    def clear(tiles, edges):
        for i, (dl, dn) in enumerate(WAYS):
            n = i - len(TILE_WAYS)

            def act(i=i, n=n):
                if n < 0:
                    tiles[i] = jnp.zeros(tiles.shape[1:], BF16)
                else:
                    edges[n] = jnp.zeros(edges.shape[1:], BF16)

            if dl:
                pl.when(jnp.logical_not(exists(-dl)))(act)

    def start(copies, ways=WAYS):
        for way, c in zip(WAYS, copies):
            if way in ways:
                when(way[0], c.start)

    def wait_recv(copies):
        for (dl, dn), c in zip(WAYS, copies):
            when(-dl, c.wait_recv)

    def wait_send(copies):
        for (dl, dn), c in zip(WAYS, copies):
            when(dl, c.wait_send)

    halo_a = halo(inp, edge_a, tiles_a, edges_a, send_a, recv_a)
    halo_b = halo(cot, edge_b, tiles_b, edges_b, send_b, recv_b)
    pays = [pltpu.make_async_remote_copy(
        src_ref=pay, dst_ref=paid.at[i], send_sem=send_c.at[i], recv_sem=recv_c.at[i],
        device_id=across(dn), device_id_type=MESH) for i, dn in enumerate((0, -1))]
    wins = [pltpu.make_async_remote_copy(
        src_ref=out_win, dst_ref=in_win.at[i], send_sem=send_d.at[i], recv_sem=recv_d.at[i],
        device_id=across(dn), device_id_type=MESH) for i, dn in enumerate((0, 1))]

    for i in range(2):
        fetch[i].wait()
        wide_raw[...] = raw[i].astype(F32)
        channels = raw.shape[1]
        for r in range(rows):
            inp[i * channels : (i + 1) * channels, r * columns : (r + 1) * columns] = (
                wide_raw[:, r, :].astype(BF16))
    pay[...] = jnp.zeros(pay.shape, F32)

    @pl.when(is_sea)
    def _():
        base = 2 * sea_k
        centre = inp[base : 2 * base, :].astype(F32)
        pay[0:1, :] = centre[0:1]
        pay[1:2, :] = centre[sea_k : sea_k + 1]

    up = jnp.where(exists(-1), 3, 0)
    down = jnp.where(exists(1), 3, 0)
    pl.semaphore_wait(barrier, 5 + up + down)
    start(halo_a, TILE_WAYS)
    edge_a[...] = pack_edges(inp[...].astype(F32), rows, columns)
    start(halo_a, EDGE_WAYS)

    @pl.when(is_sea)
    def _():
        for c in pays:
            c.start()

    clear(tiles_a, edges_a)
    clear(tiles_b, edges_b)

    for c in fetch[2:10]:
        c.wait()
    slim[...] = jnp.zeros(slim.shape, F32)
    slim[0:1, 0:air_h] = air_bias[...]
    slim[1:2, 0:sea_h] = sea_bias[...]
    slim[2:4, 0:air_k] = air_flux[...].astype(F32)
    slim[4:5, 0:air_k] = react_in[...]
    slim[5:7, 0:sea_k] = sea_force[...].astype(F32)
    par = jnp.transpose(slim[...])
    share_bias = par[0:air_h, 0:1], par[0:sea_h, 1:2]

    def lay_out_first(raw_w, w1):
        hidden, deep = raw_w.shape[2], w1.shape[1] // 3
        blank = jnp.zeros((deep - raw_w.shape[1], hidden), F32)
        for a in range(3):
            tall = jnp.concatenate([raw_w[a].astype(F32), blank], axis=0)
            w1[:, a * deep : (a + 1) * deep] = jnp.transpose(tall).astype(BF16)

    def lay_out_rest(first_raw, second_raw, w1t, w2t):
        hidden, deep = first_raw.shape[2], w2t.shape[1] // 3
        blank = jnp.zeros((deep - first_raw.shape[1], hidden), F32)
        for a in range(3):
            back = 2 - a
            tall = jnp.concatenate([second_raw[a].astype(F32), blank], axis=0)
            w2t[:, back * deep : (back + 1) * deep] = jnp.transpose(tall).astype(BF16)
            w1t[:, back * hidden : (back + 1) * hidden] = first_raw[a]

    def lay_out_second(second_raw, w2):
        hidden = second_raw.shape[2]
        for a in range(3):
            w2[:, a * hidden : (a + 1) * hidden] = second_raw[a]

    def build_table():
        index = jnp.concatenate([index_raw[:, r, :] for r in range(rows)], axis=1)
        weight = jnp.concatenate([weight_raw[:, r, :] for r in range(rows)], axis=1).astype(F32)
        near = jnp.sum(weight[0:4], axis=0, keepdims=True)
        far = jnp.sum(weight[4:8], axis=0, keepdims=True)
        slot8 = lax.broadcasted_iota(jnp.int32, weight.shape, 0)
        total = jnp.where(is_air, near + far, jnp.where(slot8 < 4, near, far))
        share = weight / total
        high = lax.shift_right_logical(index, LANES.bit_length() - 1)
        low = index & (LANES - 1)
        place = lax.broadcasted_iota(jnp.int32, (LANES, cells), 0)
        wrows = values.shape[0]
        row16 = lax.broadcasted_iota(jnp.int32, (wrows, cells), 0)
        row16 = jnp.where(is_air, row16, row16 % (wrows // 2))
        for s in range(8):
            onehot[:, s * cells : (s + 1) * cells] = jnp.where(
                place == low[s : s + 1], 1.0, 0.0).astype(BF16)
            share_hi[:, s * cells : (s + 1) * cells] = jnp.where(
                row16 == high[s : s + 1], share[s : s + 1], 0.0)

    @pl.when(is_air)
    def _():
        for c in fetch[10:12]:
            c.wait()
        lay_out_first(aw1_raw, aw1)
        lay_out_second(aw2_raw, aw2)

    @pl.when(is_sea)
    def _():
        for c in fetch[12:14]:
            c.wait()
        lay_out_first(sw1_raw, sw1)
        lay_out_second(sw2_raw, sw2)
        lay_out_rest(sw1_raw, sw2_raw, sw1t, sw2t)
        build_table()

    wrows = values.shape[0]
    per = columns // LANES

    def gather():
        for f in range(2):
            for r in range(rows):
                for nxt in range(2):
                    for h in range(per):
                        at = ((f * rows + r) * 2 + nxt) * per + h
                        lane0 = r * columns + h * LANES
                        values[at : at + 1, :] = paid[nxt, f : f + 1, lane0 : lane0 + LANES]
        got = split_dot(values[...], onehot[...], ((1,), (0,))) * share_hi[...]
        parts = [got[:, s * cells : (s + 1) * cells] for s in range(8)]
        return sum(parts[1:4], parts[0]), sum(parts[5:8], parts[4])

    def scatter(first, second):
        spread = jnp.concatenate([first] * 4 + [second] * 4, axis=1) * share_hi[...]
        out_win[...] = split_dot(spread, onehot[...], ((1,), (1,)))

    def arrived():
        fields = []
        for f in range(2):
            pieces = []
            for r in range(rows):
                for h in range(per):
                    own = ((f * rows + r) * 2) * per + h
                    pieces.append(in_win[0, own : own + 1, :] + in_win[1, own + per : own + per + 1, :])
            fields.append(jnp.concatenate(pieces, axis=1))
        return fields

    def place_of(q, split):
        height = rows * split
        where = -1 if q < 0 else (1 if q >= height else 0)
        q = q - where * height
        return where, q // rows, q % rows

    def stacks(tile, tiles, edges, base, k, split, forward, dst):
        lo, hi = base, base + k * split
        own = tile[lo:hi, :].astype(F32)
        above, below = tiles[1, lo:hi, :].astype(F32), tiles[0, lo:hi, :].astype(F32)
        sides = unpack_edges(edges)[lo:hi]
        lefts = {0: 1, -1: 5, 1: 3}
        rights = {0: 0, -1: 4, 1: 2}
        mains = {0: own, -1: above, 1: below}
        for p in range(rows * split + 4):
            where, s, r = place_of(p - 2, split)
            ch = slice(s * k, (s + 1) * k)
            row = wide_row(mains[where][ch, r * columns : (r + 1) * columns],
                           sides[ch], lefts[where], rights[where], r)
            dst[p] = jnp.concatenate(
                [three(row, forward), jnp.zeros((dst.shape[1] - 3 * k, row.shape[1]), F32)],
                axis=0).astype(BF16)

    def keep(p, height):
        gone = ((p == 0) & (lat == 0)) | ((p == height + 1) & (lat == lat_n - 1))
        return jnp.where(gone, 0.0, 1.0)

    def rows_of(ref, p):
        return ref[pl.ds(p, 3)].reshape(3 * ref.shape[1], ref.shape[2])

    def give(out, value):
        for r in range(rows):
            wide_raw[:, r, :] = value[:, r * columns : (r + 1) * columns]
        out[...] = wide_raw[...].astype(BF16)

    def first_conv(w1, bias, x, v, slope, z, height):
        def body(p, carry):
            pre = dot(w1[...], rows_of(x, p)) + bias
            t = jnp.tanh(pre)
            s = 1.0 - t * t
            slope[p] = s
            lin = dot(w1[...], rows_of(v, p))
            z[p] = (s * keep(p, height) * lin).astype(BF16)
            return carry
        lax.fori_loop(0, height + 2, body, 0)

    def second_conv(w2, z, height):
        return [fold_three(dot(w2[...], rows_of(z, i)), True, columns) for i in range(height)]

    def second_back(w2t, c, slope, z, height):
        def body(p, carry):
            lin = dot(w2t[...], rows_of(c, p))
            z[p] = (slope[p] * keep(p, height) * lin).astype(BF16)
            return carry
        lax.fori_loop(0, height + 2, body, 0)

    def first_back(w1t, z, height):
        return [fold_three(dot(w1t[...], rows_of(z, i)), False, columns) for i in range(height)]

    def packed(fine, split):
        parts = [jnp.concatenate(fine[s * rows : (s + 1) * rows], axis=1) for s in range(split)]
        return parts

    flux0, flux1 = par[0:air_k, 2:3], par[0:air_k, 3:4]
    react = par[0:air_k, 4:5]
    force0, force1 = par[0:sea_k, 5:6], par[0:sea_k, 6:7]
    half_rows = wrows // 2
    wait_recv(halo_a)

    @pl.when(is_air)
    def _():
        stacks(inp, tiles_a, edges_a, 0, air_k, 1, True, ax)
        stacks(inp, tiles_a, edges_a, air_k, air_k, 1, True, av)
        first_conv(aw1, share_bias[0], ax, av, aslope, az, rows)
        y = packed(second_conv(aw2, az, rows), 1)[0]
        pay[0:1, :] = jnp.sum(flux0 * y, axis=0, keepdims=True)
        pay[1:2, :] = jnp.sum(flux1 * y, axis=0, keepdims=True)
        for c in pays:
            c.start()
        build_table()
        lay_out_rest(aw1_raw, aw2_raw, aw1t, aw2t)
        for c in pays:
            c.wait_recv()
        near, far = gather()
        lifted = jnp.sum(near + far, axis=0, keepdims=True)
        image = (y + react * lifted).astype(BF16)
        wide = image.astype(F32)
        surface = jnp.sum(react * wide, axis=0, keepdims=True)
        source = jnp.broadcast_to(surface, (wrows, cells))
        scatter(source, source)
        for c in wins:
            c.start()
        give(image_ref, wide)
        for c in wins:
            c.wait_recv()
        back0, back1 = arrived()
        total = wide + (flux0 * back0 + flux1 * back1)
        cot[...] = total.astype(BF16)
        start(halo_b, TILE_WAYS)
        edge_b[...] = pack_edges(cot[...].astype(F32), rows, columns)

    @pl.when(is_sea)
    def _():
        stacks(inp, tiles_a, edges_a, 0, sea_k, 2, True, sx)
        stacks(inp, tiles_a, edges_a, 2 * sea_k, sea_k, 2, True, sv)
        first_conv(sw1, share_bias[1], sx, sv, sslope, sz, 2 * rows)
        ys = packed(second_conv(sw2, sz, 2 * rows), 2)
        for c in pays:
            c.wait_recv()
        images, sources = [], []
        row_at = lax.broadcasted_iota(jnp.int32, (wrows, cells), 0)
        for t, got in enumerate(gather()):
            f0 = jnp.sum(got[:half_rows], axis=0, keepdims=True)
            f1 = jnp.sum(got[half_rows:], axis=0, keepdims=True)
            mask = jnp.concatenate(
                [mask_raw[t, r : r + 1, :] for r in range(rows)], axis=1).astype(F32)
            one = (mask * (ys[t] + (force0 * f0 + force1 * f1))).astype(BF16).astype(F32)
            images.append(one)
            pulled0 = jnp.sum(force0 * one, axis=0, keepdims=True)
            pulled1 = jnp.sum(force1 * one, axis=0, keepdims=True)
            sources.append(jnp.where(row_at < half_rows, pulled0, pulled1))
        scatter(*sources)
        for c in wins:
            c.start()
        image = jnp.concatenate(images, axis=0).astype(BF16)
        cot[...] = image
        start(halo_b, TILE_WAYS)
        edge_b[...] = pack_edges(image.astype(F32), rows, columns)

    start(halo_b, EDGE_WAYS)

    @pl.when(is_sea)
    def _():
        give(image_ref, cot[...].astype(F32))

    wait_recv(halo_b)

    @pl.when(is_air)
    def _():
        stacks(cot, tiles_b, edges_b, 0, air_k, 1, False, ax)
        second_back(aw2t, ax, aslope, az, rows)
        give(product_ref, packed(first_back(aw1t, az, rows), 1)[0])

    @pl.when(is_sea)
    def _():
        stacks(cot, tiles_b, edges_b, 0, sea_k, 2, False, sx)
        second_back(sw2t, sx, sslope, sz, 2 * rows)
        fine = packed(first_back(sw1t, sz, 2 * rows), 2)
        for c in wins:
            c.wait_recv()
        top = lax.broadcasted_iota(jnp.int32, (sea_k, cells), 0) == 0
        fine = [f + jnp.where(top, b, 0.0) for f, b in zip(fine, arrived())]
        give(product_ref, jnp.concatenate(fine, axis=0))

    for c in pays + wins:
        c.wait_send()
    wait_send(halo_a)
    wait_send(halo_b)


def shards(
    lat_n, lon_n, state, direction, air_first, air_bias, air_second, air_flux, reaction,
    sea_first, sea_bias, sea_second, sea_forcing, regrid_index, regrid_weight, land_mask,
):
    channels, rows, columns = state.shape[1:]
    cells = rows * columns
    air_h, air_k = air_first.shape[1:]
    sea_h, sea_k = sea_first.shape[1:]
    def rowed(w):
        return w.reshape(3, 3 * w.shape[1], w.shape[2])

    args = [
        state[0], direction[0], regrid_index[0], regrid_weight[0], land_mask,
        air_bias[None], air_flux, reaction[None], sea_bias[None], sea_forcing.T,
        rowed(air_first.transpose(0, 2, 1)), rowed(air_second),
        rowed(sea_first.transpose(0, 2, 1)), rowed(sea_second),
    ]
    air_deep, sea_deep = 3 * air_k + -3 * air_k % LANES, 3 * sea_k + -3 * sea_k % LANES
    tall = max(air_h, sea_h)
    line_a, line_b = 2 * channels + -2 * channels % LANES, channels + -channels % LANES
    wide = columns + LANES
    wrows = 2 * rows * 2 * columns // LANES
    dma = pltpu.SemaphoreType.DMA
    vmem = pltpu.VMEM
    image, product = pl.pallas_call(
        functools.partial(kernel, (rows, columns, lat_n, lon_n, air_k, air_h, sea_k, sea_h)),
        out_shape=[jax.ShapeDtypeStruct((channels, rows, columns), BF16)] * 2,
        in_specs=[pl.BlockSpec(memory_space=pltpu.HBM)] * len(args),
        out_specs=[pl.BlockSpec(memory_space=pltpu.VMEM)] * 2,
        scratch_shapes=[
            vmem((2, channels, rows, columns), BF16),
            vmem((channels, rows, columns), F32),
            vmem(args[2].shape, jnp.int32),
            vmem(args[3].shape, jnp.int32),
            vmem(args[4].shape, jnp.int32),
            *[vmem(a.shape, a.dtype) for a in args[5:10]],
            vmem((LANES, tall), F32),
            *[vmem(a.shape, a.dtype) for a in args[10:14]],
            dma((14,)),
            vmem((air_h, 3 * air_deep), BF16),
            vmem((3 * air_k, 3 * air_h), BF16),
            vmem((3 * air_k, 3 * air_h), BF16),
            vmem((air_h, 3 * air_deep), BF16),
            vmem((sea_h, 3 * sea_deep), BF16),
            vmem((3 * sea_k, 3 * sea_h), BF16),
            vmem((3 * sea_k, 3 * sea_h), BF16),
            vmem((sea_h, 3 * sea_deep), BF16),
            vmem((2 * channels, cells), BF16),
            vmem((LINES, line_a), BF16),
            vmem((2, 2 * channels, cells), BF16),
            vmem((6, LINES, line_a), BF16),
            vmem((channels, cells), BF16),
            vmem((LINES, line_b), BF16),
            vmem((2, channels, cells), BF16),
            vmem((6, LINES, line_b), BF16),
            vmem((8, cells), F32),
            vmem((2, 8, cells), F32),
            vmem((wrows, LANES), F32),
            vmem((2, wrows, LANES), F32),
            vmem((LANES, 8 * cells), BF16),
            vmem((wrows, 8 * cells), F32),
            vmem((wrows, LANES), F32),
            vmem((rows + 4, air_deep, wide), BF16),
            vmem((rows + 4, air_deep, wide), BF16),
            vmem((rows + 2, air_h, wide), F32),
            vmem((rows + 2, air_h, wide), BF16),
            vmem((2 * rows + 4, sea_deep, wide), BF16),
            vmem((2 * rows + 4, sea_deep, wide), BF16),
            vmem((2 * rows + 2, sea_h, wide), F32),
            vmem((2 * rows + 2, sea_h, wide), BF16),
            dma((8,)), dma((8,)), dma((8,)), dma((8,)), dma((2,)), dma((2,)), dma((2,)), dma((2,)),
        ],
        compiler_params=pltpu.CompilerParams(
            collective_id=0, has_side_effects=True, vmem_limit_bytes=62 * 1024 * 1024),
        name="coupled",
    )(*args)
    return image[None], product[None]


def solution(mesh):
    field = P("comp", None, "lat", "lon")
    return jax.shard_map(
        functools.partial(shards, mesh.shape["lat"], mesh.shape["lon"]),
        mesh=mesh,
        in_specs=(field, field) + (P(),) * 9 + (field, field, P(None, "lat", "lon")),
        out_specs=(field, field),
        check_vma=False,
    )
```

```python
import functools

import jax
import jax.numpy as jnp
from jax import lax
from jax.experimental import pallas as pl
from jax.experimental.pallas import tpu as pltpu
from jax.sharding import PartitionSpec as P

MESH = pl.DeviceIdType.MESH
F32 = jnp.float32
BF16 = jnp.bfloat16
LANES = 128
LINES = 16
TILE_WAYS = ((-1, 0), (1, 0))
EDGE_WAYS = ((0, -1), (0, 1), (-1, -1), (-1, 1), (1, -1), (1, 1))
WAYS = TILE_WAYS + EDGE_WAYS


def dot(a, b):
    return jnp.dot(a, b, preferred_element_type=F32)


def split_dot(a, b, dims):
    high = a.astype(BF16)
    low = (a - high.astype(F32)).astype(BF16)
    both = lax.dot_general(
        jnp.concatenate([high, low], axis=0), b, (dims, ((), ())), preferred_element_type=F32
    )
    return both[: a.shape[0]] + both[a.shape[0] :]


def pack_edges(tile, rows, columns):
    channels = tile.shape[0]
    lane = lax.broadcasted_iota(jnp.int32, (channels, LANES), 1)
    packed = None
    for r in range(rows):
        first = tile[:, r * columns : r * columns + LANES]
        last = tile[:, (r + 1) * columns - LANES : (r + 1) * columns]
        part = jnp.where(lane < 2, first, jnp.where(lane >= LANES - 2, last, 0.0))
        part = pltpu.roll(part, 2 + 4 * r, 1)
        packed = part if packed is None else packed + part
    blank = jnp.zeros((-channels % LANES, LANES), F32)
    return jnp.transpose(jnp.concatenate([packed, blank], axis=0))[:LINES].astype(BF16)


def unpack_edges(edges):
    lines = [edges[n].astype(F32) for n in range(len(EDGE_WAYS))]
    blank = jnp.zeros((LANES - LINES * len(lines), lines[0].shape[1]), F32)
    return jnp.transpose(jnp.concatenate(lines + [blank], axis=0))


def wide_row(main, sides, left, right, r):
    lane = lax.broadcasted_iota(jnp.int32, sides.shape, 1)
    before = pltpu.roll(sides, (LANES - 2 - LINES * left - 4 * r) % LANES, 1)
    after = pltpu.roll(sides, -(LINES * right + 4 * r + 2) % LANES, 1)
    side = jnp.where(lane < 2, after, jnp.where(lane >= LANES - 2, before, 0.0))
    return jnp.concatenate([main, side], axis=1)


def three(row, forward):
    width = row.shape[1]
    before, after = pltpu.roll(row, 1, 1), pltpu.roll(row, width - 1, 1)
    parts = [before, row, after] if forward else [after, row, before]
    return jnp.concatenate(parts, axis=0)


def fold_three(stack, forward, columns):
    k = stack.shape[0] // 3
    width = stack.shape[1]
    first, mid, last = stack[:k], stack[k : 2 * k], stack[2 * k :]
    one, other = (1, width - 1) if forward else (width - 1, 1)
    return (pltpu.roll(first, one, 1) + mid + pltpu.roll(last, other, 1))[:, :columns]


def kernel(
    cfg,
    state_hbm, direction_hbm, index_hbm, weight_hbm, mask_hbm,
    air_bias_hbm, air_flux_hbm, react_hbm, sea_bias_hbm, sea_force_hbm,
    aw1_hbm, aw2_hbm, sw1_hbm, sw2_hbm,
    image_ref,
    product_ref,
    raw, wide_raw, index_raw, weight_raw, mask_raw,
    air_bias, air_flux, react_in, sea_bias, sea_force, slim,
    aw1_raw, aw2_raw, sw1_raw, sw2_raw, load,
    aw1, aw1t, aw2, aw2t,
    sw1, sw1t, sw2, sw2t,
    inp,
    edge_a, tiles_a, edges_a,
    cot, edge_b, tiles_b, edges_b,
    pay, paid, out_win, in_win,
    onehot, share_hi, values,
    ax, av, aslope, az,
    sx, sv, sslope, sz,
    send_a, recv_a, send_b, recv_b, send_c, recv_c, send_d, recv_d,
):
    rows, columns, lat_n, lon_n, air_k, air_h, sea_k, sea_h = cfg
    cells = rows * columns
    comp, lat, lon = (lax.axis_index(a) for a in ("comp", "lat", "lon"))
    is_air = comp == 0
    is_sea = comp == 1
    mine = {"comp": comp, "lat": lat, "lon": lon}
    del mine

    def exists(dl):
        return lat + dl >= 0 if dl < 0 else lat + dl < lat_n

    def there(dl, dn):
        return (comp, (lat + dl + lat_n) % lat_n, (lon + dn + lon_n) % lon_n)

    def across(dn):
        return (1 - comp, lat, (lon + dn + lon_n) % lon_n)

    def when(dl, act):
        if dl == 0:
            act()
        else:
            pl.when(exists(dl))(act)

    fetch = [pltpu.make_async_copy(src, dst, load.at[i]) for i, (src, dst) in enumerate((
        (state_hbm, raw.at[0]), (direction_hbm, raw.at[1]),
        (index_hbm, index_raw), (weight_hbm, weight_raw), (mask_hbm, mask_raw),
        (air_bias_hbm, air_bias), (air_flux_hbm, air_flux), (react_hbm, react_in),
        (sea_bias_hbm, sea_bias), (sea_force_hbm, sea_force),
        (aw1_hbm, aw1_raw), (aw2_hbm, aw2_raw), (sw1_hbm, sw1_raw), (sw2_hbm, sw2_raw)))]
    for c in fetch[:10]:
        c.start()

    @pl.when(is_air)
    def _():
        for c in fetch[10:12]:
            c.start()

    @pl.when(is_sea)
    def _():
        for c in fetch[12:14]:
            c.start()

    barrier = pltpu.get_barrier_semaphore()
    for dl, dn in WAYS:
        when(dl, lambda dl=dl, dn=dn: pl.semaphore_signal(
            barrier, inc=1, device_id=there(dl, dn), device_id_type=MESH))
    for dn in (-1, 0, 1):
        pl.semaphore_signal(barrier, inc=1, device_id=across(dn), device_id_type=MESH)

    def halo(tile, edge, tiles, edges, send, recv):
        copies = []
        for i, (dl, dn) in enumerate(WAYS):
            n = i - len(TILE_WAYS)
            copies.append(pltpu.make_async_remote_copy(
                src_ref=tile if n < 0 else edge,
                dst_ref=tiles.at[i] if n < 0 else edges.at[n],
                send_sem=send.at[i], recv_sem=recv.at[i],
                device_id=there(dl, dn), device_id_type=MESH))
        return copies

    def clear(tiles, edges):
        for i, (dl, dn) in enumerate(WAYS):
            n = i - len(TILE_WAYS)

            def act(i=i, n=n):
                if n < 0:
                    tiles[i] = jnp.zeros(tiles.shape[1:], BF16)
                else:
                    edges[n] = jnp.zeros(edges.shape[1:], BF16)

            if dl:
                pl.when(jnp.logical_not(exists(-dl)))(act)

    def start(copies, ways=WAYS):
        for way, c in zip(WAYS, copies):
            if way in ways:
                when(way[0], c.start)

    def wait_recv(copies):
        for (dl, dn), c in zip(WAYS, copies):
            when(-dl, c.wait_recv)

    def wait_send(copies):
        for (dl, dn), c in zip(WAYS, copies):
            when(dl, c.wait_send)

    halo_a = halo(inp, edge_a, tiles_a, edges_a, send_a, recv_a)
    halo_b = halo(cot, edge_b, tiles_b, edges_b, send_b, recv_b)
    pays = [pltpu.make_async_remote_copy(
        src_ref=pay, dst_ref=paid.at[i], send_sem=send_c.at[i], recv_sem=recv_c.at[i],
        device_id=across(dn), device_id_type=MESH) for i, dn in enumerate((0, -1))]
    wins = [pltpu.make_async_remote_copy(
        src_ref=out_win, dst_ref=in_win.at[i], send_sem=send_d.at[i], recv_sem=recv_d.at[i],
        device_id=across(dn), device_id_type=MESH) for i, dn in enumerate((0, 1))]

    for i in range(2):
        fetch[i].wait()
        wide_raw[...] = raw[i].astype(F32)
        channels = raw.shape[1]
        for r in range(rows):
            inp[i * channels : (i + 1) * channels, r * columns : (r + 1) * columns] = (
                wide_raw[:, r, :].astype(BF16))
    pay[...] = jnp.zeros(pay.shape, F32)

    @pl.when(is_sea)
    def _():
        base = 2 * sea_k
        centre = inp[base : 2 * base, :].astype(F32)
        pay[0:1, :] = centre[0:1]
        pay[1:2, :] = centre[sea_k : sea_k + 1]

    up = jnp.where(exists(-1), 3, 0)
    down = jnp.where(exists(1), 3, 0)
    pl.semaphore_wait(barrier, 5 + up + down)
    start(halo_a, TILE_WAYS)
    edge_a[...] = pack_edges(inp[...].astype(F32), rows, columns)
    start(halo_a, EDGE_WAYS)

    @pl.when(is_sea)
    def _():
        for c in pays:
            c.start()

    clear(tiles_a, edges_a)
    clear(tiles_b, edges_b)

    for c in fetch[2:10]:
        c.wait()
    slim[...] = jnp.zeros(slim.shape, F32)
    slim[0:1, 0:air_h] = air_bias[...]
    slim[1:2, 0:sea_h] = sea_bias[...]
    slim[2:4, 0:air_k] = air_flux[...].astype(F32)
    slim[4:5, 0:air_k] = react_in[...]
    slim[5:7, 0:sea_k] = sea_force[...].astype(F32)
    par = jnp.transpose(slim[...])
    share_bias = par[0:air_h, 0:1], par[0:sea_h, 1:2]

    def lay_out_first(raw_w, w1):
        hidden, deep = raw_w.shape[2], w1.shape[1] // 3
        blank = jnp.zeros((deep - raw_w.shape[1], hidden), F32)
        for a in range(3):
            tall = jnp.concatenate([raw_w[a].astype(F32), blank], axis=0)
            w1[:, a * deep : (a + 1) * deep] = jnp.transpose(tall).astype(BF16)

    def lay_out_rest(first_raw, second_raw, w1t, w2t):
        hidden, deep = first_raw.shape[2], w2t.shape[1] // 3
        blank = jnp.zeros((deep - first_raw.shape[1], hidden), F32)
        for a in range(3):
            back = 2 - a
            tall = jnp.concatenate([second_raw[a].astype(F32), blank], axis=0)
            w2t[:, back * deep : (back + 1) * deep] = jnp.transpose(tall).astype(BF16)
            w1t[:, back * hidden : (back + 1) * hidden] = first_raw[a]

    def lay_out_second(second_raw, w2):
        hidden = second_raw.shape[2]
        for a in range(3):
            w2[:, a * hidden : (a + 1) * hidden] = second_raw[a]

    def build_table():
        index = jnp.concatenate([index_raw[:, r, :] for r in range(rows)], axis=1)
        weight = jnp.concatenate([weight_raw[:, r, :] for r in range(rows)], axis=1).astype(F32)
        near = jnp.sum(weight[0:4], axis=0, keepdims=True)
        far = jnp.sum(weight[4:8], axis=0, keepdims=True)
        slot8 = lax.broadcasted_iota(jnp.int32, weight.shape, 0)
        total = jnp.where(is_air, near + far, jnp.where(slot8 < 4, near, far))
        share = weight / total
        high = lax.shift_right_logical(index, LANES.bit_length() - 1)
        low = index & (LANES - 1)
        place = lax.broadcasted_iota(jnp.int32, (LANES, cells), 0)
        wrows = values.shape[0]
        row16 = lax.broadcasted_iota(jnp.int32, (wrows, cells), 0)
        row16 = jnp.where(is_air, row16, row16 % (wrows // 2))
        for s in range(8):
            onehot[:, s * cells : (s + 1) * cells] = jnp.where(
                place == low[s : s + 1], 1.0, 0.0).astype(BF16)
            share_hi[:, s * cells : (s + 1) * cells] = jnp.where(
                row16 == high[s : s + 1], share[s : s + 1], 0.0)

    @pl.when(is_air)
    def _():
        for c in fetch[10:12]:
            c.wait()
        lay_out_first(aw1_raw, aw1)
        lay_out_second(aw2_raw, aw2)

    @pl.when(is_sea)
    def _():
        for c in fetch[12:14]:
            c.wait()
        lay_out_first(sw1_raw, sw1)
        lay_out_second(sw2_raw, sw2)
        lay_out_rest(sw1_raw, sw2_raw, sw1t, sw2t)
        build_table()

    wrows = values.shape[0]
    per = columns // LANES

    def gather():
        for f in range(2):
            for r in range(rows):
                for nxt in range(2):
                    for h in range(per):
                        at = ((f * rows + r) * 2 + nxt) * per + h
                        lane0 = r * columns + h * LANES
                        values[at : at + 1, :] = paid[nxt, f : f + 1, lane0 : lane0 + LANES]
        got = split_dot(values[...], onehot[...], ((1,), (0,))) * share_hi[...]
        parts = [got[:, s * cells : (s + 1) * cells] for s in range(8)]
        return sum(parts[1:4], parts[0]), sum(parts[5:8], parts[4])

    def scatter(first, second):
        spread = jnp.concatenate([first] * 4 + [second] * 4, axis=1) * share_hi[...]
        out_win[...] = split_dot(spread, onehot[...], ((1,), (1,)))

    def arrived():
        fields = []
        for f in range(2):
            pieces = []
            for r in range(rows):
                for h in range(per):
                    own = ((f * rows + r) * 2) * per + h
                    pieces.append(in_win[0, own : own + 1, :] + in_win[1, own + per : own + per + 1, :])
            fields.append(jnp.concatenate(pieces, axis=1))
        return fields

    def place_of(q, split):
        height = rows * split
        where = -1 if q < 0 else (1 if q >= height else 0)
        q = q - where * height
        return where, q // rows, q % rows

    def stacks(tile, tiles, edges, base, k, split, forward, dst):
        lo, hi = base, base + k * split
        own = tile[lo:hi, :].astype(F32)
        above, below = tiles[1, lo:hi, :].astype(F32), tiles[0, lo:hi, :].astype(F32)
        sides = unpack_edges(edges)[lo:hi]
        lefts = {0: 1, -1: 5, 1: 3}
        rights = {0: 0, -1: 4, 1: 2}
        mains = {0: own, -1: above, 1: below}
        for p in range(rows * split + 4):
            where, s, r = place_of(p - 2, split)
            ch = slice(s * k, (s + 1) * k)
            row = wide_row(mains[where][ch, r * columns : (r + 1) * columns],
                           sides[ch], lefts[where], rights[where], r)
            dst[p] = jnp.concatenate(
                [three(row, forward), jnp.zeros((dst.shape[1] - 3 * k, row.shape[1]), F32)],
                axis=0).astype(BF16)

    def keep(p, height):
        gone = ((p == 0) & (lat == 0)) | ((p == height + 1) & (lat == lat_n - 1))
        return jnp.where(gone, 0.0, 1.0)

    def rows_of(ref, p):
        return ref[pl.ds(p, 3)].reshape(3 * ref.shape[1], ref.shape[2])

    def give(out, value):
        for r in range(rows):
            wide_raw[:, r, :] = value[:, r * columns : (r + 1) * columns]
        out[...] = wide_raw[...].astype(BF16)

    def first_conv(w1, bias, x, v, slope, z, height):
        def body(p, carry):
            both = dot(w1[...], jnp.concatenate([rows_of(x, p), rows_of(v, p)], axis=1))
            width = x.shape[2]
            pre, lin = both[:, :width] + bias, both[:, width:]
            t = jnp.tanh(pre)
            s = 1.0 - t * t
            slope[p] = s
            z[p] = (s * keep(p, height) * lin).astype(BF16)
            return carry
        lax.fori_loop(0, height + 2, body, 0)

    def two_rows(w, z, height, forward):
        out, width = [], z.shape[2]
        for i in range(0, height, 2):
            both = dot(w[...], jnp.concatenate([rows_of(z, i), rows_of(z, i + 1)], axis=1))
            out += [fold_three(both[:, :width], forward, columns),
                    fold_three(both[:, width:], forward, columns)]
        return out

    def second_conv(w2, z, height):
        return two_rows(w2, z, height, True)

    def second_back(w2t, c, slope, z, height):
        def body(pair, carry):
            p, width = 2 * pair, c.shape[2]
            both = dot(w2t[...], jnp.concatenate([rows_of(c, p), rows_of(c, p + 1)], axis=1))
            z[p] = (slope[p] * keep(p, height) * both[:, :width]).astype(BF16)
            z[p + 1] = (slope[p + 1] * keep(p + 1, height) * both[:, width:]).astype(BF16)
            return carry
        lax.fori_loop(0, (height + 2) // 2, body, 0)

    def first_back(w1t, z, height):
        return two_rows(w1t, z, height, False)

    def packed(fine, split):
        parts = [jnp.concatenate(fine[s * rows : (s + 1) * rows], axis=1) for s in range(split)]
        return parts

    flux0, flux1 = par[0:air_k, 2:3], par[0:air_k, 3:4]
    react = par[0:air_k, 4:5]
    force0, force1 = par[0:sea_k, 5:6], par[0:sea_k, 6:7]
    half_rows = wrows // 2
    wait_recv(halo_a)

    @pl.when(is_air)
    def _():
        stacks(inp, tiles_a, edges_a, 0, air_k, 1, True, ax)
        stacks(inp, tiles_a, edges_a, air_k, air_k, 1, True, av)
        first_conv(aw1, share_bias[0], ax, av, aslope, az, rows)
        y = packed(second_conv(aw2, az, rows), 1)[0]
        pay[0:1, :] = jnp.sum(flux0 * y, axis=0, keepdims=True)
        pay[1:2, :] = jnp.sum(flux1 * y, axis=0, keepdims=True)
        for c in pays:
            c.start()
        build_table()
        lay_out_rest(aw1_raw, aw2_raw, aw1t, aw2t)
        for c in pays:
            c.wait_recv()
        near, far = gather()
        lifted = jnp.sum(near + far, axis=0, keepdims=True)
        image = (y + react * lifted).astype(BF16)
        wide = image.astype(F32)
        surface = jnp.sum(react * wide, axis=0, keepdims=True)
        source = jnp.broadcast_to(surface, (wrows, cells))
        scatter(source, source)
        for c in wins:
            c.start()
        give(image_ref, wide)
        for c in wins:
            c.wait_recv()
        back0, back1 = arrived()
        total = wide + (flux0 * back0 + flux1 * back1)
        cot[...] = total.astype(BF16)
        start(halo_b, TILE_WAYS)
        edge_b[...] = pack_edges(cot[...].astype(F32), rows, columns)

    @pl.when(is_sea)
    def _():
        stacks(inp, tiles_a, edges_a, 0, sea_k, 2, True, sx)
        stacks(inp, tiles_a, edges_a, 2 * sea_k, sea_k, 2, True, sv)
        first_conv(sw1, share_bias[1], sx, sv, sslope, sz, 2 * rows)
        ys = packed(second_conv(sw2, sz, 2 * rows), 2)
        for c in pays:
            c.wait_recv()
        images, sources = [], []
        row_at = lax.broadcasted_iota(jnp.int32, (wrows, cells), 0)
        for t, got in enumerate(gather()):
            f0 = jnp.sum(got[:half_rows], axis=0, keepdims=True)
            f1 = jnp.sum(got[half_rows:], axis=0, keepdims=True)
            mask = jnp.concatenate(
                [mask_raw[t, r : r + 1, :] for r in range(rows)], axis=1).astype(F32)
            one = (mask * (ys[t] + (force0 * f0 + force1 * f1))).astype(BF16).astype(F32)
            images.append(one)
            pulled0 = jnp.sum(force0 * one, axis=0, keepdims=True)
            pulled1 = jnp.sum(force1 * one, axis=0, keepdims=True)
            sources.append(jnp.where(row_at < half_rows, pulled0, pulled1))
        scatter(*sources)
        for c in wins:
            c.start()
        image = jnp.concatenate(images, axis=0).astype(BF16)
        cot[...] = image
        start(halo_b, TILE_WAYS)
        edge_b[...] = pack_edges(image.astype(F32), rows, columns)

    start(halo_b, EDGE_WAYS)

    @pl.when(is_sea)
    def _():
        give(image_ref, cot[...].astype(F32))

    wait_recv(halo_b)

    @pl.when(is_air)
    def _():
        stacks(cot, tiles_b, edges_b, 0, air_k, 1, False, ax)
        second_back(aw2t, ax, aslope, az, rows)
        give(product_ref, packed(first_back(aw1t, az, rows), 1)[0])

    @pl.when(is_sea)
    def _():
        stacks(cot, tiles_b, edges_b, 0, sea_k, 2, False, sx)
        second_back(sw2t, sx, sslope, sz, 2 * rows)
        fine = packed(first_back(sw1t, sz, 2 * rows), 2)
        for c in wins:
            c.wait_recv()
        top = lax.broadcasted_iota(jnp.int32, (sea_k, cells), 0) == 0
        fine = [f + jnp.where(top, b, 0.0) for f, b in zip(fine, arrived())]
        give(product_ref, jnp.concatenate(fine, axis=0))

    for c in pays + wins:
        c.wait_send()
    wait_send(halo_a)
    wait_send(halo_b)


def shards(
    lat_n, lon_n, state, direction, air_first, air_bias, air_second, air_flux, reaction,
    sea_first, sea_bias, sea_second, sea_forcing, regrid_index, regrid_weight, land_mask,
):
    channels, rows, columns = state.shape[1:]
    cells = rows * columns
    air_h, air_k = air_first.shape[1:]
    sea_h, sea_k = sea_first.shape[1:]
    def rowed(w):
        return w.reshape(3, 3 * w.shape[1], w.shape[2])

    args = [
        state[0], direction[0], regrid_index[0], regrid_weight[0], land_mask,
        air_bias[None], air_flux, reaction[None], sea_bias[None], sea_forcing.T,
        rowed(air_first.transpose(0, 2, 1)), rowed(air_second),
        rowed(sea_first.transpose(0, 2, 1)), rowed(sea_second),
    ]
    air_deep, sea_deep = 3 * air_k + -3 * air_k % LANES, 3 * sea_k + -3 * sea_k % LANES
    tall = max(air_h, sea_h)
    line_a, line_b = 2 * channels + -2 * channels % LANES, channels + -channels % LANES
    wide = columns + LANES
    wrows = 2 * rows * 2 * columns // LANES
    dma = pltpu.SemaphoreType.DMA
    vmem = pltpu.VMEM
    image, product = pl.pallas_call(
        functools.partial(kernel, (rows, columns, lat_n, lon_n, air_k, air_h, sea_k, sea_h)),
        out_shape=[jax.ShapeDtypeStruct((channels, rows, columns), BF16)] * 2,
        in_specs=[pl.BlockSpec(memory_space=pltpu.HBM)] * len(args),
        out_specs=[pl.BlockSpec(memory_space=pltpu.VMEM)] * 2,
        scratch_shapes=[
            vmem((2, channels, rows, columns), BF16),
            vmem((channels, rows, columns), F32),
            vmem(args[2].shape, jnp.int32),
            vmem(args[3].shape, jnp.int32),
            vmem(args[4].shape, jnp.int32),
            *[vmem(a.shape, a.dtype) for a in args[5:10]],
            vmem((LANES, tall), F32),
            *[vmem(a.shape, a.dtype) for a in args[10:14]],
            dma((14,)),
            vmem((air_h, 3 * air_deep), BF16),
            vmem((3 * air_k, 3 * air_h), BF16),
            vmem((3 * air_k, 3 * air_h), BF16),
            vmem((air_h, 3 * air_deep), BF16),
            vmem((sea_h, 3 * sea_deep), BF16),
            vmem((3 * sea_k, 3 * sea_h), BF16),
            vmem((3 * sea_k, 3 * sea_h), BF16),
            vmem((sea_h, 3 * sea_deep), BF16),
            vmem((2 * channels, cells), BF16),
            vmem((LINES, line_a), BF16),
            vmem((2, 2 * channels, cells), BF16),
            vmem((6, LINES, line_a), BF16),
            vmem((channels, cells), BF16),
            vmem((LINES, line_b), BF16),
            vmem((2, channels, cells), BF16),
            vmem((6, LINES, line_b), BF16),
            vmem((8, cells), F32),
            vmem((2, 8, cells), F32),
            vmem((wrows, LANES), F32),
            vmem((2, wrows, LANES), F32),
            vmem((LANES, 8 * cells), BF16),
            vmem((wrows, 8 * cells), F32),
            vmem((wrows, LANES), F32),
            vmem((rows + 4, air_deep, wide), BF16),
            vmem((rows + 4, air_deep, wide), BF16),
            vmem((rows + 2, air_h, wide), F32),
            vmem((rows + 2, air_h, wide), BF16),
            vmem((2 * rows + 4, sea_deep, wide), BF16),
            vmem((2 * rows + 4, sea_deep, wide), BF16),
            vmem((2 * rows + 2, sea_h, wide), F32),
            vmem((2 * rows + 2, sea_h, wide), BF16),
            dma((8,)), dma((8,)), dma((8,)), dma((8,)), dma((2,)), dma((2,)), dma((2,)), dma((2,)),
        ],
        compiler_params=pltpu.CompilerParams(
            collective_id=0, has_side_effects=True, vmem_limit_bytes=62 * 1024 * 1024),
        name="coupled",
    )(*args)
    return image[None], product[None]


def solution(mesh):
    field = P("comp", None, "lat", "lon")
    return jax.shard_map(
        functools.partial(shards, mesh.shape["lat"], mesh.shape["lon"]),
        mesh=mesh,
        in_specs=(field, field) + (P(),) * 9 + (field, field, P(None, "lat", "lon")),
        out_specs=(field, field),
        check_vma=False,
    )
```
